32 devices in a mesh: parts: 2 (over x), wide: 16 (over z, y, core).
Axes of the slice: x: 2, y: 2, z: 4, core: 2. Of those that a mesh axis runs over, the one named last changes fastest.
Arguments:
- voxels: bfloat16 [32768, 256], P(('parts', 'wide')), parts along dimension 0, may hold values from -16 to 16
- regular_window: int32 [32768], P(('parts', 'wide')), parts along dimension 0, may hold values from 0 to 127, never falling along the last dimension, each value on 1 to 256 neighbouring positions
- shifted_window: int32 [32768], P(('parts', 'wide')), parts along dimension 0, may hold values from 0 to 127, never falling along the last dimension, each value on 1 to 256 neighbouring positions
- dest: int32 [32768], P(('parts', 'wide')), parts along dimension 0, may hold values from 0 to 16383, as said below
- w_qkv: bfloat16 [2, 256, 768], replicated, may hold values from -0.375 to 0.375
- w_out: bfloat16 [2, 256, 256], replicated, may hold values from -1.5 to 1.5
- gain: float32 [2, 256], replicated, may hold values from 0.1 to 1.9
- temper: float32 [2, 8], replicated, may hold values from 0.5 to 6
Outputs:
- shifted_out: bfloat16 [32768, 256], P(('parts', 'wide')), parts along dimension 0
The draws below stay inside these ranges and needn't reach their ends.
There are 2 independent parts, one for each index of `parts`. The reference program is written for one: setup_inputs(seed, part) draws one part's arguments, and reference() takes and returns one part's arrays. A program takes and returns all parts, laid end to end along the dimension named above; an argument that names none is the same for every part. Nothing has to cross between parts.
Inputs may be any that keep to these rules, and one draw needn't show every extreme that they name: `regular_window`: window ids never fall along the order; every window has 1 to 256 voxels and one has exactly 256. `shifted_window`: window ids never fall along the order; every window has 1 to 256 voxels and one has exactly 256. dest is a permutation. Counting blocks of 1024 consecutive positions, at most 128 voxels go from one block of the regular order to one block of the shifted order, and some pair reaches 128; the count from a block to the block k places further along, cyclically, is the same for every block.
All inputs are finite; a program needn't handle non-finite values.
Results may differ from the reference program's by a relative error of at most 0.007.
The reference program's roundings to bfloat16 on the way (of `projected`, `weights`, `attended`, `sublayer`, `first` and `moved`) count: a program that leaves them out, or rounds other values in their place, can miss the bound.
Values may be sent and summed in bfloat16 or wider, within the bound.
No kernel may reach another device: no remote copies, remote signals or barrier semaphores. Data moves between devices by JAX's collectives and lax.ppermute only.
A program may use at most 64 MiB of HBM per device.

```python
import math
import jax
import jax.numpy as jnp
import numpy as np
from jax import lax

C = 256
HEADS = 8
VOX_DEV = 1024
WIN = 256
VOXELS = 16384
WINDOWS = 128


def draw_voxels(key, part):
    first_key = jax.random.fold_in(key, 0)
    base = jax.random.normal(first_key, (VOXELS, C), jnp.float32)
    values = jnp.clip(base, -6.0, 6.0)
    return values.astype(jnp.bfloat16)


def draw_temper(key, part):
    uniforms = jax.random.uniform(key, (2, HEADS), jnp.float32)
    values = jnp.exp(math.log(0.5) + uniforms * math.log(8.0))
    return values.astype(jnp.float32)


def draw_dest(key, part):
    groups = VOXELS // VOX_DEV
    share = VOX_DEV // groups
    first_key, second_key, third_key, fourth_key = jax.random.split(key, 4)
    lifts = jax.random.randint(first_key, (groups // 2,), 0, share + 1).astype(jnp.int32)
    lifts = lifts.at[0].set(share)
    amounts = jnp.stack([share + lifts, share - lifts], axis=1).reshape(groups)
    amounts = amounts[jax.random.permutation(second_key, groups)]
    bounds = jnp.cumsum(amounts).astype(jnp.int32)
    local_order = jax.vmap(lambda one_key: jax.random.permutation(one_key, VOX_DEV))(jax.random.split(third_key, groups))
    local_order = local_order.astype(jnp.int32)
    offsets = jnp.sum((bounds[None, None, :] <= local_order[:, :, None]).astype(jnp.int32), axis=2)
    target = (jnp.arange(groups, dtype=jnp.int32)[:, None] + offsets) % groups
    arrival = jax.vmap(lambda one_key: jax.random.permutation(one_key, VOX_DEV))(jax.random.split(fourth_key, groups))
    arrival = arrival.astype(jnp.int32)
    final_slot = arrival[target, local_order]
    return (target * VOX_DEV + final_slot).reshape(VOXELS).astype(jnp.int32)


def profile(count, total, reach, slope):
    weights = [(1 << 20) // math.isqrt(standing ** slope) + 1 for standing in range(2, count + 1)]
    spare, counts = total - reach - (count - 1), [1] * (count - 1)
    while spare > 0:
        movable = [i for i in range(count - 1) if counts[i] < reach]
        whole, budget = sum([weights[i] for i in movable]), spare
        for i in movable:
            extra = min(reach - counts[i], max(1, budget * weights[i] // whole), spare)
            counts[i] = counts[i] + extra
            spare = spare - extra
    return np.array([reach] + counts)


def uneven_parts(own_key, number_of, total, bound, lean):
    if number_of == 2:
        one = jax.random.randint(own_key, (), max(1, total - bound), min(bound, total - 1) + 1)
        return jnp.stack([one, total - one])
    tallies = jnp.asarray(profile(number_of, total, bound, lean), jnp.int32)
    pairs = (number_of - 1) // 2
    source_of, sink = tallies[1:1 + 2 * pairs:2], tallies[2:2 + 2 * pairs:2]
    room = jnp.minimum(source_of - 1, bound - sink)
    shifted = jax.random.randint(jax.random.fold_in(own_key, 1), (pairs,), 0, 1 << 20) % (room + 1)
    tallies = tallies.at[1:1 + 2 * pairs:2].set(source_of - shifted).at[2:2 + 2 * pairs:2].set(sink + shifted)
    return tallies[jax.random.permutation(jax.random.fold_in(own_key, 2), number_of)]


def centred(key, dims, width, bound, kind=jnp.bfloat16):
    return jnp.clip(width * jax.random.normal(key, dims, jnp.float32), -bound, bound).astype(kind)


def setup_inputs(seed: int = 0, part: int = 0) -> dict:
    keys = jax.random.split(jax.random.key(seed), 9)
    part_keys = jax.random.split(jax.random.fold_in(keys[8], part), 9)
    voxels = draw_voxels(jax.random.fold_in(jax.random.fold_in(keys[8], part), 71), part)
    regular_window = jnp.searchsorted(jnp.cumsum(uneven_parts(part_keys[1], WINDOWS, VOXELS, WIN, 1)), jnp.arange(VOXELS), side="right").astype(jnp.int32)
    shifted_window = jnp.searchsorted(jnp.cumsum(uneven_parts(part_keys[2], WINDOWS, VOXELS, WIN, 1)), jnp.arange(VOXELS), side="right").astype(jnp.int32)
    dest = draw_dest(jax.random.fold_in(jax.random.fold_in(keys[8], part), 71), part)
    w_qkv = centred(keys[4], (2, C, 3 * C), C ** -0.5, 0.375)
    w_out = centred(keys[5], (2, C, C), (C // 16) ** -0.5, 1.5)
    gain = jnp.clip(1.0 + 0.18 * jax.random.normal(keys[6], (2, C), jnp.float32), 0.1, 1.9)
    temper = draw_temper(jax.random.fold_in(keys[8], 71), part)
    return {"voxels": voxels, "regular_window": regular_window, "shifted_window": shifted_window, "dest": dest, "w_qkv": w_qkv, "w_out": w_out, "gain": gain, "temper": temper}


epsilon = 1e-05
masked_score = -1e+30

def settle(hidden, attended, w_out_layer, gain_layer):
    summed = hidden.astype(jnp.float32) + jnp.dot(attended, w_out_layer, preferred_element_type=jnp.float32)
    center = lax.optimization_barrier(jnp.mean(summed, axis=1, keepdims=True))
    spread = lax.optimization_barrier(jnp.mean(jnp.square(summed - center), axis=1, keepdims=True))
    return ((summed - center) * lax.rsqrt(spread + epsilon) * gain_layer).astype(jnp.bfloat16)

def sublayer(hidden, window_ids, w_qkv_layer, w_out_layer, gain_layer, temper_layer):
    total_rows = hidden.shape[0]
    channels = hidden.shape[1]
    head_dim = channels // HEADS
    projected = jnp.dot(hidden, w_qkv_layer, preferred_element_type=jnp.float32).astype(jnp.bfloat16)
    queries = projected[:, :channels]
    padded = jnp.pad(projected[:, channels:], ((WIN, WIN), (0, 0)))
    marks = (window_ids + 1).astype(jnp.int32)
    marks_pad = jnp.pad(marks, (WIN, WIN))
    factor = temper_layer * (1.0 / math.sqrt(head_dim))
    block_rows = math.gcd(total_rows, 512)
    key_rows = block_rows + 2 * WIN

    def one_block(number):
        first_row = (number * block_rows).astype(jnp.int32)
        query_block = lax.dynamic_slice_in_dim(queries, first_row, block_rows, 0).astype(jnp.float32)
        query_block = query_block.reshape(block_rows, HEADS, head_dim)
        key_block = lax.dynamic_slice_in_dim(padded, first_row, key_rows, 0).astype(jnp.float32)
        keys_part = key_block[:, :channels].reshape(key_rows, HEADS, head_dim)
        values_part = key_block[:, channels:].reshape(key_rows, HEADS, head_dim)
        mark_query = lax.dynamic_slice_in_dim(marks, first_row, block_rows, 0)
        mark_key = lax.dynamic_slice_in_dim(marks_pad, first_row, key_rows, 0)
        same_window = (mark_query[:, None] == mark_key[None, :])[None]
        scores = jnp.einsum('qhd,khd->hqk', query_block, keys_part) * factor[:, None, None]
        scores = jnp.where(same_window, scores, masked_score)
        highest = lax.optimization_barrier(jnp.max(scores, axis=2, keepdims=True))
        exponents = jnp.where(same_window, jnp.exp(scores - highest), 0.0)
        totals = lax.optimization_barrier(jnp.sum(exponents, axis=2, keepdims=True))
        weights = (exponents / totals).astype(jnp.bfloat16)
        result = jnp.einsum('hqk,khd->qhd', weights.astype(jnp.float32), values_part)
        return result.reshape(block_rows, channels).astype(jnp.bfloat16)
    attended = lax.map(one_block, jnp.arange(total_rows // block_rows, dtype=jnp.int32))
    attended = attended.reshape(total_rows, channels)
    return settle(hidden, attended, w_out_layer, gain_layer)

def reference(voxels, regular_window, shifted_window, dest, w_qkv, w_out, gain, temper):
    first = sublayer(voxels, regular_window, w_qkv[0], w_out[0], gain[0], temper[0])
    moved = jnp.zeros_like(first).at[dest.astype(jnp.int32)].set(first)
    return sublayer(moved, shifted_window, w_qkv[1], w_out[1], gain[1], temper[1])
```

```python
import functools
import math

import jax
import jax.numpy as jnp
from jax import lax
from jax.experimental import pallas as pl
from jax.experimental.pallas import tpu as pltpu
from jax.sharding import PartitionSpec as P

HEADS = 8
TILE = 128

epsilon = 1e-05
masked_score = -1e30
no_mark = 1 << 30

vmem = pl.BlockSpec(memory_space=pltpu.VMEM)
smem = pl.BlockSpec(memory_space=pltpu.SMEM)


def dot(a, b):
    return jnp.dot(a, b, preferred_element_type=jnp.float32)


def dot_t(a, b):
    return lax.dot_general(a, b, (((1,), (1,)), ((), ())), preferred_element_type=jnp.float32)


def ranks(match):
    rows, columns = match.shape
    before = (
        lax.broadcasted_iota(jnp.int32, (TILE, TILE), 0)
        < lax.broadcasted_iota(jnp.int32, (TILE, TILE), 1)
    ).astype(jnp.bfloat16)
    carry = jnp.zeros((rows, 1), jnp.float32)
    pieces = []
    for start in range(0, columns, TILE):
        piece = match[:, start : start + TILE]
        pieces.append(dot(piece.astype(jnp.bfloat16), before) + carry)
        carry = carry + jnp.sum(piece, axis=1, keepdims=True)
    return jnp.concatenate(pieces, axis=1)


def one_hot(hits):
    return jnp.where(hits, 1.0, 0.0).astype(jnp.bfloat16)


def attend_tile(number, span_ref, scale_ref, marks_ref, query_ref, keyval_ref, attended_ref, rim):
    channels = query_ref.shape[1]
    head_dim = channels // HEADS
    per_group = TILE // head_dim
    groups = channels // TILE
    row = pl.multiple_of(number * TILE, TILE)
    low = span_ref[0, number]
    count = span_ref[1, number]
    most = 1 + 2 * (rim // TILE)
    lane_head = lax.broadcasted_iota(jnp.int32, (TILE, TILE), 1) // head_dim
    own = marks_ref[pl.ds(number + rim // TILE, 1), :]
    own = jnp.transpose(jnp.broadcast_to(own, (TILE, TILE)))

    def variant(tiles):
        first_key = pl.multiple_of(low * TILE, TILE)
        same = [own == marks_ref[pl.ds(low + i, 1), :] for i in range(tiles)]
        same = jnp.concatenate(same, axis=1)
        for group in range(groups):
            lanes = slice(group * TILE, (group + 1) * TILE)
            query = query_ref[pl.ds(row, TILE), lanes]
            stacked = jnp.concatenate(
                [jnp.where(lane_head == j, query, 0.0).astype(jnp.bfloat16) for j in range(per_group)],
                axis=0,
            )
            keys = keyval_ref[pl.ds(first_key, tiles * TILE), lanes]
            values = keyval_ref[
                pl.ds(first_key, tiles * TILE),
                channels + group * TILE : channels + (group + 1) * TILE,
            ]
            scores = dot_t(stacked, keys)
            weights = []
            for j in range(per_group):
                part = scores[j * TILE : (j + 1) * TILE] * scale_ref[group * per_group + j]
                part = jnp.where(same, part, masked_score)
                part = jnp.exp2(part - jnp.max(part, axis=1, keepdims=True))
                part = part * (1.0 / jnp.sum(part, axis=1, keepdims=True))
                weights.append(part.astype(jnp.bfloat16))
            mixed = dot(jnp.concatenate(weights, axis=0), values)
            total = mixed[:TILE]
            for j in range(1, per_group):
                total = jnp.where(lane_head == j, mixed[j * TILE : (j + 1) * TILE], total)
            attended_ref[pl.ds(row, TILE), lanes] = total.astype(jnp.bfloat16)

    for tiles in range(2, most + 1):
        pl.when(jnp.maximum(count, 2) == tiles)(functools.partial(variant, tiles))


def sublayer_kernel(
    packing, span_ref, scale_ref, marks_ref, dest_ref, low_ref, hidden_ref, high_ref, w_qkv_ref,
    w_out_ref, gain_ref, out_ref, query_ref, keyval_ref, attended_ref, first_ref,
):
    rows, channels = hidden_ref.shape
    rim = low_ref.shape[0]
    chunk = min(256, rows)
    for start in range(0, rows, chunk):
        projected = dot(hidden_ref[start : start + chunk], w_qkv_ref[...]).astype(jnp.bfloat16)
        query_ref[start : start + chunk] = projected[:, :channels]
        keyval_ref[rim + start : rim + start + chunk] = projected[:, channels:]
    keyval_ref[:rim] = dot(low_ref[...], w_qkv_ref[:, channels:]).astype(jnp.bfloat16)
    keyval_ref[rim + rows :] = dot(high_ref[...], w_qkv_ref[:, channels:]).astype(jnp.bfloat16)

    def one_tile(number, nothing):
        attend_tile(
            number, span_ref, scale_ref, marks_ref, query_ref, keyval_ref, attended_ref, rim
        )
        return nothing

    lax.fori_loop(0, rows // TILE, one_tile, 0)
    final_ref = first_ref if packing else out_ref
    for start in range(0, rows, chunk):
        here = slice(start, start + chunk)
        summed = hidden_ref[here].astype(jnp.float32) + dot(attended_ref[here], w_out_ref[...])
        center = jnp.mean(summed, axis=1, keepdims=True)
        summed = summed - center
        spread = jnp.mean(jnp.square(summed), axis=1, keepdims=True)
        final_ref[here] = (summed * lax.rsqrt(spread + epsilon) * gain_ref[...]).astype(jnp.bfloat16)
    if not packing:
        return
    devices = packing
    capacity = 2 * rows // devices
    target = dest_ref[...] // rows
    match = jnp.where(
        lax.broadcasted_iota(jnp.int32, (devices, rows), 0) == target, 1.0, 0.0
    )
    place = jnp.sum(ranks(match) * match, axis=0, keepdims=True).astype(jnp.int32)
    place = place + target * capacity
    for start in range(0, devices * capacity, TILE):
        index = lax.broadcasted_iota(jnp.int32, (TILE, rows), 0) + start
        out_ref[start : start + TILE] = dot(one_hot(index == place), first_ref[...]).astype(
            jnp.bfloat16
        )


def run_sublayer(hidden, low, high, marks, spans, dest, w_qkv, w_out, gain, temper, packing):
    rows, channels = hidden.shape
    rim = low.shape[0]
    scale = temper * (1.0 / math.sqrt(channels // HEADS)) * math.log2(math.e)
    out_rows = 2 * rows if packing else rows
    return pl.pallas_call(
        functools.partial(sublayer_kernel, packing),
        out_shape=jax.ShapeDtypeStruct((out_rows, channels), jnp.bfloat16),
        in_specs=[smem, smem] + [vmem] * 8,
        out_specs=vmem,
        scratch_shapes=[
            pltpu.VMEM((rows, channels), jnp.bfloat16),
            pltpu.VMEM((rows + 2 * rim, 2 * channels), jnp.bfloat16),
            pltpu.VMEM((rows, channels), jnp.bfloat16),
            pltpu.VMEM((rows, channels), jnp.bfloat16),
        ],
        compiler_params=pltpu.CompilerParams(vmem_limit_bytes=40 * 1024 * 1024),
        cost_estimate=pl.CostEstimate(
            flops=8 * 10**9, bytes_accessed=4 * 10**6, transcendentals=8 * 10**6
        ),
        name="sublayer",
    )(
        spans, scale, marks.reshape(-1, TILE), dest.reshape(1, rows), low, hidden, high, w_qkv,
        w_out, gain.reshape(1, channels),
    )


def slots_kernel(capacity, base_ref, dest_ref, slots_ref):
    devices, rows = dest_ref.shape
    slot = dest_ref[...] - base_ref[0]
    inside = (slot >= 0) & (slot < rows)
    match = jnp.where(inside, 1.0, 0.0)
    rank = jnp.where(inside, ranks(match).astype(jnp.int32), -1)
    slot = jnp.where(inside, slot, 0)
    which = lax.broadcasted_iota(jnp.int32, (16, rows), 0)
    place = lax.broadcasted_iota(jnp.int32, (capacity, rows), 0)
    for source in range(devices):
        own = slot[source : source + 1]
        digits = jnp.where(
            which == 0, own // 32, jnp.where(which == 1, own % 32, jnp.where(which == 2, 1, 0))
        )
        hits = one_hot(place == rank[source : source + 1])
        found = dot_t(digits.astype(jnp.float32).astype(jnp.bfloat16), hits)
        value = found[0:1] * 32.0 + found[1:2] + (found[2:3] - 1.0) * 2048.0
        slots_ref[source : source + 1] = value.astype(jnp.int32)


def run_slots(base, dest_all, capacity):
    devices = dest_all.shape[0]
    return pl.pallas_call(
        functools.partial(slots_kernel, capacity),
        out_shape=jax.ShapeDtypeStruct((devices, capacity), jnp.int32),
        in_specs=[smem, vmem],
        out_specs=vmem,
        compiler_params=pltpu.CompilerParams(vmem_limit_bytes=40 * 1024 * 1024),
        cost_estimate=pl.CostEstimate(flops=2 * 10**9, bytes_accessed=10**6, transcendentals=0),
        name="slots",
    )(base, dest_all)


def place_kernel(slots_ref, arrived_ref, moved_ref):
    rows = moved_ref.shape[0]
    parts = slots_ref.shape[0]
    for start in range(0, rows, TILE):
        index = lax.broadcasted_iota(jnp.int32, (TILE, TILE), 0) + start
        hits = jnp.concatenate([one_hot(index == slots_ref[i : i + 1]) for i in range(parts)], axis=1)
        moved_ref[start : start + TILE] = dot(hits, arrived_ref[...]).astype(jnp.bfloat16)


def run_place(slots, arrived, rows):
    return pl.pallas_call(
        place_kernel,
        out_shape=jax.ShapeDtypeStruct((rows, arrived.shape[1]), jnp.bfloat16),
        in_specs=[vmem, vmem],
        out_specs=vmem,
        compiler_params=pltpu.CompilerParams(vmem_limit_bytes=40 * 1024 * 1024),
        cost_estimate=pl.CostEstimate(
            flops=10**9, bytes_accessed=2 * 10**6, transcendentals=0
        ),
        name="place",
    )(slots.reshape(-1, TILE), arrived)


def neighbours(block, width, axis):
    count = lax.axis_size("wide")
    forward = [(i, i + 1) for i in range(count - 1)]
    backward = [(target, source) for source, target in forward]
    size = block.shape[axis]
    low = lax.ppermute(lax.slice_in_dim(block, size - width, size, axis=axis), "wide", forward)
    high = lax.ppermute(lax.slice_in_dim(block, 0, width, axis=axis), "wide", backward)
    return low, high


def extents(marks, low, high):
    high = jnp.where(high == 0, no_mark, high)
    padded = jnp.concatenate([low, marks, high])
    begin = jnp.sum((padded[None, :] < marks[::TILE, None]).astype(jnp.int32), axis=1) // TILE
    end = jnp.sum((padded[None, :] <= marks[TILE - 1 :: TILE, None]).astype(jnp.int32), axis=1)
    end = (end + TILE - 1) // TILE
    return padded, jnp.stack([begin, end - begin])


def body(voxels, regular_window, shifted_window, dest, w_qkv, w_out, gain, temper):
    rows, channels = voxels.shape
    rim = rows // 4
    devices = lax.axis_size("wide")
    capacity = 2 * rows // devices
    base = lax.axis_index("wide").astype(jnp.int32).reshape(1) * rows
    low, high = neighbours(voxels, rim, 0)
    marks = jnp.stack([regular_window, shifted_window]) + 1
    marks_low, marks_high = neighbours(marks, rim, 1)
    dest_all = lax.all_gather(dest, "wide")
    marks_first, spans_first = extents(marks[0], marks_low[0], marks_high[0])
    marks_second, spans_second = extents(marks[1], marks_low[1], marks_high[1])
    outgoing = run_sublayer(
        voxels, low, high, marks_first, spans_first, dest, w_qkv[0], w_out[0], gain[0], temper[0],
        devices,
    )
    arrived = lax.all_to_all(outgoing, "wide", split_axis=0, concat_axis=0, tiled=True)
    slots = run_slots(base, dest_all, capacity)
    moved = run_place(slots, arrived, rows)
    low, high = neighbours(moved, rim, 0)
    return run_sublayer(
        moved, low, high, marks_second, spans_second, dest, w_qkv[1], w_out[1], gain[1], temper[1],
        0,
    )


def solution(mesh):
    in_specs = (
        P(("parts", "wide"), None),
        P(("parts", "wide")),
        P(("parts", "wide")),
        P(("parts", "wide")),
        P(),
        P(),
        P(),
        P(),
    )
    out_specs = P(("parts", "wide"), None)
    return jax.shard_map(body, mesh=mesh, in_specs=in_specs, out_specs=out_specs, check_vma=False)
```

```python
import functools
import math

import jax
import jax.numpy as jnp
from jax import lax
from jax.experimental import pallas as pl
from jax.experimental.pallas import tpu as pltpu
from jax.sharding import PartitionSpec as P

HEADS = 8
TILE = 128
TAIL = 16

epsilon = 1e-05
masked_score = -1e30
no_mark = 1 << 30
vmem_limit = 40 * 1024 * 1024

vmem = pl.BlockSpec(memory_space=pltpu.VMEM)
smem = pl.BlockSpec(memory_space=pltpu.SMEM)


def dot(a, b):
    return jnp.dot(a, b, preferred_element_type=jnp.float32)


def dot_t(a, b):
    return lax.dot_general(a, b, (((1,), (1,)), ((), ())), preferred_element_type=jnp.float32)


def one_hot(hits):
    return jnp.where(hits, 1.0, 0.0).astype(jnp.bfloat16)


def ranks(match):
    rows, columns = match.shape
    before = one_hot(
        lax.broadcasted_iota(jnp.int32, (TILE, TILE), 0)
        < lax.broadcasted_iota(jnp.int32, (TILE, TILE), 1)
    )
    carry = jnp.zeros((rows, 1), jnp.float32)
    pieces = []
    for start in range(0, columns, TILE):
        piece = match[:, start : start + TILE]
        pieces.append(dot(piece.astype(jnp.bfloat16), before) + carry)
        carry = carry + jnp.sum(piece, axis=1, keepdims=True)
    return jnp.concatenate(pieces, axis=1)


def project_kernel(layer, hidden_ref, w_qkv_ref, query_ref, key_ref, value_ref):
    rows, channels = hidden_ref.shape
    chunk = min(256, rows)
    w_value = jnp.transpose(w_qkv_ref[layer, :, 2 * channels :])
    for start in range(0, rows, chunk):
        here = slice(start, start + chunk)
        both = dot(hidden_ref[here], w_qkv_ref[layer, :, : 2 * channels]).astype(jnp.bfloat16)
        query_ref[here] = both[:, :channels]
        key_ref[here] = both[:, channels:]
        value_ref[:, here] = dot_t(w_value, hidden_ref[here]).astype(jnp.bfloat16)


def run_project(layer, hidden, w_qkv):
    rows, channels = hidden.shape
    return pl.pallas_call(
        functools.partial(project_kernel, layer),
        out_shape=(
            jax.ShapeDtypeStruct((rows, channels), jnp.bfloat16),
            jax.ShapeDtypeStruct((rows, channels), jnp.bfloat16),
            jax.ShapeDtypeStruct((channels, rows), jnp.bfloat16),
        ),
        in_specs=[vmem, vmem],
        out_specs=(vmem, vmem, vmem),
        compiler_params=pltpu.CompilerParams(vmem_limit_bytes=vmem_limit),
        cost_estimate=pl.CostEstimate(
            flops=6 * rows * channels * channels, bytes_accessed=3 * 10**6, transcendentals=0
        ),
        name="project",
    )(hidden, w_qkv)


def attend_tile(
    number, span_ref, scales, marks_ref, column_ref, query_ref, key_ref, value_ref, attended_ref,
    rim,
):
    channels = query_ref.shape[1]
    head_dim = channels // HEADS
    per_group = TILE // head_dim
    groups = channels // TILE
    row = pl.multiple_of(number * TILE, TILE)
    low = span_ref[0, number]
    count = span_ref[1, number]
    most = 1 + 2 * (rim // TILE)
    lane_head = lax.broadcasted_iota(jnp.int32, (TILE, TILE), 1) // head_dim

    def variant(tiles):
        first_key = pl.multiple_of(low * TILE, TILE)
        span = pl.ds(first_key, tiles * TILE)
        own = marks_ref[pl.ds(number + rim // TILE, 1), :]
        bias = jnp.where(column_ref[span, :] == own, 0.0, masked_score)
        for group in range(groups):
            lanes = slice(group * TILE, (group + 1) * TILE)
            query = query_ref[pl.ds(row, TILE), lanes]
            stacked = jnp.concatenate(
                [jnp.where(lane_head == j, query, 0.0).astype(jnp.bfloat16) for j in range(per_group)],
                axis=0,
            )
            scores = dot_t(key_ref[span, lanes], stacked)
            for pair in range(0, per_group, 2):
                weights = []
                for j in (pair, pair + 1):
                    part = scores[:, j * TILE : (j + 1) * TILE] * scales[group * per_group + j]
                    part = part + bias
                    part = jnp.exp2(part - jnp.max(part, axis=0, keepdims=True))
                    part = part * (1.0 / jnp.sum(part, axis=0, keepdims=True))
                    weights.append(part.astype(jnp.bfloat16))
                begin = group * TILE + pair * head_dim
                mixed = dot(
                    value_ref[begin : begin + 2 * head_dim, span], jnp.concatenate(weights, axis=1)
                )
                attended_ref[pl.ds(number, 1), begin : begin + head_dim] = mixed[:head_dim, :TILE][None]
                attended_ref[pl.ds(number, 1), begin + head_dim : begin + 2 * head_dim] = mixed[
                    head_dim:, TILE:
                ][None]

    for tiles in range(2, most + 1):
        pl.when(jnp.maximum(count, 2) == tiles)(functools.partial(variant, tiles))


def halo_marks(tail_ref, layer, rim):
    channels = tail_ref.shape[1]
    found = []
    for start in range(0, rim, TILE):
        digits = []
        for digit in range(2):
            place = (2 * layer + digit) * rim + start
            line, lane = rim + place // channels, place % channels
            digits.append(tail_ref[rim : rim + TAIL, lane : lane + TILE].astype(jnp.float32)[line - rim : line - rim + 1])
        found.append((digits[0] * 256.0 + digits[1]).astype(jnp.int32))
    return found


def sublayer_kernel(
    layer, packing, temper_ref, window_ref, dest_ref, marks_own_ref, low_tail_ref, high_tail_ref,
    low_ref, hidden_ref, high_ref, query_ref, key_own_ref, value_own_ref, w_qkv_ref, w_out_ref,
    gain_ref, out_ref, span_ref, marks_ref, column_ref, key_ref, value_ref, attended_ref, first_ref,
):
    rows, channels = hidden_ref.shape
    rim = rows // 4
    rim_tiles, own_tiles = rim // TILE, rows // TILE
    factor = (1.0 / math.sqrt(channels // HEADS)) * math.log2(math.e)
    scales = [temper_ref[layer, j] * factor for j in range(HEADS)]

    low_marks = halo_marks(low_tail_ref, layer, rim)
    high_marks = [jnp.where(m == 0, no_mark, m) for m in halo_marks(high_tail_ref, layer, rim)]
    for i in range(rim_tiles):
        marks_ref[i : i + 1] = low_marks[i]
        marks_ref[rim_tiles + own_tiles + i : rim_tiles + own_tiles + i + 1] = high_marks[i]
    marks_ref[rim_tiles : rim_tiles + own_tiles] = marks_own_ref[...] + 1
    lasts = [jnp.max(m) for m in low_marks]
    firsts = [jnp.min(m) for m in high_marks]
    own_first = [window_ref[i * TILE] + 1 for i in range(own_tiles)]
    own_last = [window_ref[(i + 1) * TILE - 1] + 1 for i in range(own_tiles)]
    for t in range(own_tiles):
        begin = jnp.int32(0)
        for mark in lasts + own_last[:t]:
            begin += (mark < own_first[t]).astype(jnp.int32)
        end = jnp.int32(rim_tiles + t + 1)
        for mark in own_first[t + 1 :] + firsts:
            end += (mark <= own_last[t]).astype(jnp.int32)
        span_ref[0, t] = begin
        span_ref[1, t] = end - begin
    for i in range(2 * rim_tiles + own_tiles):
        column_ref[i * TILE : (i + 1) * TILE] = jnp.transpose(
            jnp.broadcast_to(marks_ref[i : i + 1, :], (TILE, TILE))
        )

    w_value = jnp.transpose(w_qkv_ref[layer, :, 2 * channels :])
    key_ref[rim : rim + rows] = key_own_ref[...]
    value_ref[:, rim : rim + rows] = value_own_ref[...]
    for source, start in ((low_ref, 0), (high_ref, rim + rows)):
        source = source[:rim]
        key_ref[start : start + rim] = dot(
            source, w_qkv_ref[layer, :, channels : 2 * channels]
        ).astype(jnp.bfloat16)
        value_ref[:, start : start + rim] = dot_t(w_value, source).astype(jnp.bfloat16)

    def one_tile(number, nothing):
        attend_tile(
            number, span_ref, scales, marks_ref, column_ref, query_ref, key_ref, value_ref,
            attended_ref, rim,
        )
        return nothing

    lax.fori_loop(0, own_tiles, one_tile, 0)
    final_ref = first_ref if packing else out_ref
    for number in range(own_tiles):
        here = slice(number * TILE, (number + 1) * TILE)
        attended = jnp.transpose(attended_ref[number]).astype(jnp.bfloat16)
        summed = hidden_ref[here].astype(jnp.float32) + dot(attended, w_out_ref[layer])
        center = jnp.mean(summed, axis=1, keepdims=True)
        summed = summed - center
        spread = jnp.mean(jnp.square(summed), axis=1, keepdims=True)
        scaled = summed * lax.rsqrt(spread + epsilon) * gain_ref[layer : layer + 1]
        final_ref[here] = scaled.astype(jnp.bfloat16)
    if packing:
        pack(packing, dest_ref, first_ref, out_ref)


def pack(devices, dest_ref, first_ref, out_ref):
    rows, channels = first_ref.shape
    capacity = 2 * rows // devices
    dest = jnp.concatenate([dest_ref[i : i + 1] for i in range(rows // TILE)], axis=1)
    target = dest // rows
    match = jnp.where(lax.broadcasted_iota(jnp.int32, (devices, rows), 0) == target, 1.0, 0.0)
    place = jnp.sum(ranks(match) * match, axis=0, keepdims=True).astype(jnp.int32)
    place = place + target * capacity
    slot = dest - target * rows
    which = lax.broadcasted_iota(jnp.int32, (TAIL, rows), 0)
    digits = jnp.where(
        which == 0, slot // 32 + 1, jnp.where(which == 1, slot % 32, 0)
    )
    digits = digits.astype(jnp.float32).astype(jnp.bfloat16)
    together = max(1, 512 // capacity)
    index = lax.broadcasted_iota(jnp.int32, (together * capacity, rows), 0)
    for start in range(0, devices, together):
        hits = one_hot(index == place - start * capacity)
        packed = dot(hits, first_ref[...]).astype(jnp.bfloat16)
        slots = dot_t(digits, hits)
        for i in range(together):
            here = slice(i * capacity, (i + 1) * capacity)
            out_ref[start + i, :capacity] = packed[here]
            mine = slots[:, here]
            if capacity < TILE:
                blank = jnp.zeros((TAIL, TILE - capacity), jnp.float32)
                mine = jnp.concatenate([mine, blank], axis=1)
            extra = jnp.concatenate([mine[0:8], pltpu.roll(mine[0:8], 7, 0)], axis=1)
            out_ref[start + i, capacity:] = extra.astype(jnp.bfloat16)


def run_sublayer(layer, packing, temper, window, dest, tails, low, hidden, high, w_qkv, w_out, gain):
    rows, channels = hidden.shape
    rim = rows // 4
    tiles = rows // TILE
    seen = rows + 2 * rim
    projected = run_project(layer, hidden, w_qkv)
    shape = (packing, 2 * rows // packing + 8, channels) if packing else (rows, channels)
    return pl.pallas_call(
        functools.partial(sublayer_kernel, layer, packing),
        out_shape=jax.ShapeDtypeStruct(shape, jnp.bfloat16),
        in_specs=[smem, smem] + [vmem] * 13,
        out_specs=vmem,
        scratch_shapes=[
            pltpu.SMEM((2, tiles), jnp.int32),
            pltpu.VMEM((seen // TILE, TILE), jnp.int32),
            pltpu.VMEM((seen, TILE), jnp.int32),
            pltpu.VMEM((seen, channels), jnp.bfloat16),
            pltpu.VMEM((channels, seen), jnp.bfloat16),
            pltpu.VMEM((tiles, channels, TILE), jnp.float32),
            pltpu.VMEM((rows, channels), jnp.bfloat16),
        ],
        compiler_params=pltpu.CompilerParams(vmem_limit_bytes=vmem_limit),
        cost_estimate=pl.CostEstimate(
            flops=8 * 10**9, bytes_accessed=4 * 10**6, transcendentals=8 * 10**6
        ),
        name="sublayer",
    )(
        temper, window, dest.reshape(tiles, TILE), window.reshape(tiles, TILE), *tails, low, hidden,
        high, *projected, w_qkv, w_out, gain,
    )


def place_kernel(arrived_ref, moved_ref):
    rows = moved_ref.shape[0]
    devices, padded, channels = arrived_ref.shape
    capacity = padded - 8
    slots = []
    for i in range(devices):
        line = arrived_ref[i, capacity:].astype(jnp.float32)
        value = line[0:1, :capacity] * 32.0 + line[0:1, TILE : TILE + capacity] - 32.0
        slots.append(value.astype(jnp.int32))
    arrived = jnp.concatenate([arrived_ref[i, :capacity] for i in range(devices)], axis=0)
    chunk = min(256, rows)
    for start in range(0, rows, chunk):
        index = lax.broadcasted_iota(jnp.int32, (chunk, capacity), 0) + start
        hits = jnp.concatenate([one_hot(index == slots[i]) for i in range(devices)], axis=1)
        moved_ref[start : start + chunk] = dot(hits, arrived).astype(jnp.bfloat16)


def run_place(arrived, rows):
    return pl.pallas_call(
        place_kernel,
        out_shape=jax.ShapeDtypeStruct((rows, arrived.shape[2]), jnp.bfloat16),
        in_specs=[vmem],
        out_specs=vmem,
        compiler_params=pltpu.CompilerParams(vmem_limit_bytes=vmem_limit),
        cost_estimate=pl.CostEstimate(
            flops=10**9, bytes_accessed=2 * 10**6, transcendentals=0
        ),
        name="place",
    )(arrived)


def exchange(to_right, to_left):
    count = lax.axis_size("wide")
    forward = [(i, i + 1) for i in range(count - 1)]
    backward = [(target, source) for source, target in forward]
    return lax.ppermute(to_right, "wide", forward), lax.ppermute(to_left, "wide", backward)


def with_marks(features, windows):
    channels = features.shape[1]
    marks = windows + 1
    digits = jnp.stack([marks // 256, marks % 256], axis=1).reshape(-1)
    digits = jnp.pad(digits, (0, TAIL * channels - digits.shape[0])).reshape(TAIL, channels)
    return jnp.concatenate([features, digits.astype(jnp.bfloat16)], axis=0)


def body(voxels, regular_window, shifted_window, dest, w_qkv, w_out, gain, temper):
    rows, channels = voxels.shape
    rim = rows // 4
    devices = lax.axis_size("wide")
    windows = jnp.stack([regular_window, shifted_window])
    tails = exchange(
        with_marks(voxels[rows - rim :], windows[:, rows - rim :]),
        with_marks(voxels[:rim], windows[:, :rim]),
    )
    outgoing = run_sublayer(
        0, devices, temper, regular_window, dest, tails, tails[0], voxels, tails[1], w_qkv, w_out,
        gain,
    )
    arrived = lax.all_to_all(outgoing, "wide", split_axis=0, concat_axis=0, tiled=True)
    moved = run_place(arrived, rows)
    low, high = exchange(moved[rows - rim :], moved[:rim])
    return run_sublayer(
        1, 0, temper, shifted_window, dest, tails, low, moved, high, w_qkv, w_out, gain
    )


def solution(mesh):
    in_specs = (
        P(("parts", "wide"), None),
        P(("parts", "wide")),
        P(("parts", "wide")),
        P(("parts", "wide")),
        P(),
        P(),
        P(),
        P(),
    )
    out_specs = P(("parts", "wide"), None)
    return jax.shard_map(body, mesh=mesh, in_specs=in_specs, out_specs=out_specs, check_vma=False)
```

```python
import functools
import math

import jax
import jax.numpy as jnp
from jax import lax
from jax.experimental import pallas as pl
from jax.experimental.pallas import tpu as pltpu
from jax.sharding import PartitionSpec as P

HEADS = 8
TILE = 128
TAIL = 16

epsilon = 1e-05
masked_score = -1e30
no_mark = 1 << 30
vmem_limit = 40 * 1024 * 1024

vmem = pl.BlockSpec(memory_space=pltpu.VMEM)
smem = pl.BlockSpec(memory_space=pltpu.SMEM)


def dot(a, b):
    return jnp.dot(a, b, preferred_element_type=jnp.float32)


def dot_t(a, b):
    return lax.dot_general(a, b, (((1,), (1,)), ((), ())), preferred_element_type=jnp.float32)


def one_hot(hits):
    return jnp.where(hits, 1.0, 0.0).astype(jnp.bfloat16)


def ranks(match):
    rows, columns = match.shape
    before = one_hot(
        lax.broadcasted_iota(jnp.int32, (TILE, TILE), 0)
        < lax.broadcasted_iota(jnp.int32, (TILE, TILE), 1)
    )
    carry = jnp.zeros((rows, 1), jnp.float32)
    pieces = []
    for start in range(0, columns, TILE):
        piece = match[:, start : start + TILE]
        pieces.append(dot(piece.astype(jnp.bfloat16), before) + carry)
        carry = carry + jnp.sum(piece, axis=1, keepdims=True)
    return jnp.concatenate(pieces, axis=1)


def project_kernel(layer, hidden_ref, w_qkv_ref, query_ref, key_ref, value_ref):
    rows, channels = hidden_ref.shape
    chunk = min(256, rows)
    w_query = jnp.transpose(w_qkv_ref[layer, :, :channels])
    w_value = jnp.transpose(w_qkv_ref[layer, :, 2 * channels :])
    w_both = jnp.concatenate([w_query, w_value], axis=0)
    for start in range(0, rows, chunk):
        here = slice(start, start + chunk)
        source = hidden_ref[here]
        key_ref[here] = dot(source, w_qkv_ref[layer, :, channels : 2 * channels]).astype(
            jnp.bfloat16
        )
        both = dot_t(w_both, source).astype(jnp.bfloat16)
        query_ref[:, here] = both[:channels]
        value_ref[:, here] = both[channels:]


def run_project(layer, hidden, w_qkv):
    rows, channels = hidden.shape
    return pl.pallas_call(
        functools.partial(project_kernel, layer),
        out_shape=(
            jax.ShapeDtypeStruct((channels, rows), jnp.bfloat16),
            jax.ShapeDtypeStruct((rows, channels), jnp.bfloat16),
            jax.ShapeDtypeStruct((channels, rows), jnp.bfloat16),
        ),
        in_specs=[vmem, vmem],
        out_specs=(vmem, vmem, vmem),
        compiler_params=pltpu.CompilerParams(vmem_limit_bytes=vmem_limit),
        cost_estimate=pl.CostEstimate(
            flops=6 * rows * channels * channels, bytes_accessed=3 * 10**6, transcendentals=0
        ),
        name="project",
    )(hidden, w_qkv)


def attend_tile(
    number, span_ref, scales, marks_ref, column_ref, query_ref, key_ref, value_ref, attended_ref,
    rim,
):
    channels = query_ref.shape[0]
    head_dim = channels // HEADS
    per_group = TILE // head_dim
    groups = channels // TILE
    row = pl.multiple_of(number * TILE, TILE)
    low = span_ref[0, number]
    count = span_ref[1, number]
    most = 1 + 2 * (rim // TILE)
    blank = jnp.zeros((head_dim, TILE), jnp.bfloat16)

    def variant(tiles):
        first_key = pl.multiple_of(low * TILE, TILE)
        span = pl.ds(first_key, tiles * TILE)
        own = marks_ref[pl.ds(number + rim // TILE, 1), :]
        bias = jnp.where(column_ref[span, :] == own, 0.0, masked_score)
        parts = []
        for j in range(HEADS):
            group = j * head_dim // TILE
            column = [blank] * per_group
            column[j % per_group] = query_ref[j * head_dim : (j + 1) * head_dim, pl.ds(row, TILE)]
            keys = key_ref[span, group * TILE : (group + 1) * TILE]
            parts.append(dot(keys, jnp.concatenate(column, axis=0)))
        weights = []
        for j in range(HEADS):
            part = parts[j] * scales[j] + bias
            part = jnp.exp2(part - jnp.max(part, axis=0, keepdims=True))
            part = part * (1.0 / jnp.sum(part, axis=0, keepdims=True))
            weights.append(part.astype(jnp.bfloat16))
        for j in range(HEADS):
            begin = j * head_dim
            mixed = dot(value_ref[begin : begin + head_dim, span], weights[j])
            attended_ref[pl.ds(number, 1), begin : begin + head_dim] = mixed[None]

    for tiles in range(2, most + 1):
        pl.when(jnp.maximum(count, 2) == tiles)(functools.partial(variant, tiles))


def mark_place(layer, digit, start, rim, channels):
    place = (2 * layer + digit) * rim + start
    return place // channels, place % channels


def halo_marks(tail, layer, rim):
    found = []
    for start in range(0, rim, TILE):
        digits = []
        for digit in range(2):
            line, lane = mark_place(layer, digit, start, rim, tail.shape[1])
            digits.append(tail[line : line + 1, lane : lane + TILE])
        found.append((digits[0] * 256.0 + digits[1]).astype(jnp.int32))
    return found


def tail_of(windows_refs, first_tile, rim, channels):
    which = lax.broadcasted_iota(jnp.int32, (TAIL, TILE), 0)
    columns = [jnp.zeros((TAIL, TILE), jnp.float32) for _ in range(channels // TILE)]
    for layer, window_ref in enumerate(windows_refs):
        for start in range(0, rim, TILE):
            mark = window_ref[pl.ds(first_tile + start // TILE, 1), :] + 1
            for digit, value in enumerate((mark // 256, mark % 256)):
                line, lane = mark_place(layer, digit, start, rim, channels)
                column = columns[lane // TILE]
                columns[lane // TILE] = jnp.where(which == line, value.astype(jnp.float32), column)
    return jnp.concatenate(columns, axis=1).astype(jnp.bfloat16)


def edges_kernel(odd_ref, hidden_ref, regular_ref, shifted_ref, near_ref, far_ref):
    rows, channels = hidden_ref.shape
    rim = rows // 4
    for out_ref, at_end in ((near_ref, 1 - odd_ref[0]), (far_ref, odd_ref[0])):
        start = pl.multiple_of(at_end * (rows - rim), TILE)
        out_ref[:rim] = hidden_ref[pl.ds(start, rim)]
        out_ref[rim:] = tail_of(
            (regular_ref, shifted_ref), at_end * ((rows - rim) // TILE), rim, channels
        )


def run_edges(odd, hidden, regular, shifted):
    rows, channels = hidden.shape
    shape = jax.ShapeDtypeStruct((rows // 4 + TAIL, channels), jnp.bfloat16)
    return pl.pallas_call(
        edges_kernel,
        out_shape=(shape, shape),
        in_specs=[smem, vmem, vmem, vmem],
        out_specs=(vmem, vmem),
        name="edges",
    )(odd, hidden, regular.reshape(-1, TILE), shifted.reshape(-1, TILE))


def sublayer_kernel(
    layer, packing, odd_ref, temper_ref, window_ref, dest_ref, marks_own_ref, near_tail_ref,
    far_tail_ref, near_ref, hidden_ref, far_ref, query_ref, key_own_ref, value_own_ref, w_qkv_ref, w_out_ref,
    gain_ref, out_ref, span_ref, marks_ref, column_ref, key_ref, value_ref, attended_ref, first_ref,
):
    rows, channels = hidden_ref.shape
    rim = rows // 4
    rim_tiles, own_tiles = rim // TILE, rows // TILE
    factor = (1.0 / math.sqrt(channels // HEADS)) * math.log2(math.e)
    scales = [temper_ref[layer, j] * factor for j in range(HEADS)]

    odd = odd_ref[0]
    near_tail = near_tail_ref[rim : rim + TAIL].astype(jnp.float32)
    far_tail = far_tail_ref[rim : rim + TAIL].astype(jnp.float32)
    is_odd = jnp.full(near_tail.shape, odd, jnp.int32) == 1
    low_marks = halo_marks(jnp.where(is_odd, near_tail, far_tail), layer, rim)
    high_marks = halo_marks(jnp.where(is_odd, far_tail, near_tail), layer, rim)
    high_marks = [jnp.where(m == 0, no_mark, m) for m in high_marks]
    for i in range(rim_tiles):
        marks_ref[i : i + 1] = low_marks[i]
        marks_ref[rim_tiles + own_tiles + i : rim_tiles + own_tiles + i + 1] = high_marks[i]
    marks_ref[rim_tiles : rim_tiles + own_tiles] = marks_own_ref[...] + 1
    lasts = [jnp.max(m) for m in low_marks]
    firsts = [jnp.min(m) for m in high_marks]
    own_first = [window_ref[i * TILE] + 1 for i in range(own_tiles)]
    own_last = [window_ref[(i + 1) * TILE - 1] + 1 for i in range(own_tiles)]
    for t in range(own_tiles):
        begin = jnp.int32(0)
        for mark in lasts + own_last[:t]:
            begin += (mark < own_first[t]).astype(jnp.int32)
        end = jnp.int32(rim_tiles + t + 1)
        for mark in own_first[t + 1 :] + firsts:
            end += (mark <= own_last[t]).astype(jnp.int32)
        span_ref[0, t] = begin
        span_ref[1, t] = end - begin
    for i in range(2 * rim_tiles + own_tiles):
        column_ref[i * TILE : (i + 1) * TILE] = jnp.transpose(
            jnp.broadcast_to(marks_ref[i : i + 1, :], (TILE, TILE))
        )

    w_value = jnp.transpose(w_qkv_ref[layer, :, 2 * channels :])
    key_ref[rim : rim + rows] = key_own_ref[...]
    value_ref[:, rim : rim + rows] = value_own_ref[...]
    for source, at_end in ((near_ref, 1 - odd), (far_ref, odd)):
        source = source[:rim]
        there = pl.ds(pl.multiple_of(at_end * (rim + rows), TILE), rim)
        key_ref[there] = dot(source, w_qkv_ref[layer, :, channels : 2 * channels]).astype(
            jnp.bfloat16
        )
        value_ref[:, there] = dot_t(w_value, source).astype(jnp.bfloat16)

    def one_tile(number, nothing):
        attend_tile(
            number, span_ref, scales, marks_ref, column_ref, query_ref, key_ref, value_ref,
            attended_ref, rim,
        )
        return nothing

    lax.fori_loop(0, own_tiles, one_tile, 0)
    final_ref = first_ref if packing else out_ref
    for number in range(own_tiles):
        here = slice(number * TILE, (number + 1) * TILE)
        attended = jnp.transpose(attended_ref[number]).astype(jnp.bfloat16)
        summed = hidden_ref[here].astype(jnp.float32) + dot(attended, w_out_ref[layer])
        center = jnp.mean(summed, axis=1, keepdims=True)
        summed = summed - center
        spread = jnp.mean(jnp.square(summed), axis=1, keepdims=True)
        scaled = summed * lax.rsqrt(spread + epsilon) * gain_ref[layer : layer + 1]
        final_ref[here] = scaled.astype(jnp.bfloat16)
    if packing:
        pack(packing, dest_ref, first_ref, out_ref)


def pack(devices, dest_ref, first_ref, out_ref):
    rows, channels = first_ref.shape
    capacity = 2 * rows // devices
    dest = jnp.concatenate([dest_ref[i : i + 1] for i in range(rows // TILE)], axis=1)
    target = dest // rows
    match = jnp.where(lax.broadcasted_iota(jnp.int32, (devices, rows), 0) == target, 1.0, 0.0)
    place = jnp.sum(ranks(match) * match, axis=0, keepdims=True).astype(jnp.int32)
    place = place + target * capacity
    slot = dest - target * rows
    which = lax.broadcasted_iota(jnp.int32, (TAIL, rows), 0)
    digits = jnp.where(
        which == 0, slot // 32 + 1, jnp.where(which == 1, slot % 32, 0)
    )
    digits = digits.astype(jnp.float32).astype(jnp.bfloat16)
    together = max(1, 512 // capacity)
    index = lax.broadcasted_iota(jnp.int32, (together * capacity, rows), 0)
    for start in range(0, devices, together):
        hits = one_hot(index == place - start * capacity)
        packed = dot(hits, first_ref[...]).astype(jnp.bfloat16)
        slots = dot_t(digits, hits)
        for i in range(together):
            here = slice(i * capacity, (i + 1) * capacity)
            out_ref[start + i, :capacity] = packed[here]
            mine = slots[:, here]
            if capacity < TILE:
                blank = jnp.zeros((TAIL, TILE - capacity), jnp.float32)
                mine = jnp.concatenate([mine, blank], axis=1)
            extra = jnp.concatenate([mine[0:8], pltpu.roll(mine[0:8], 7, 0)], axis=1)
            out_ref[start + i, capacity:] = extra.astype(jnp.bfloat16)


def run_sublayer(
    layer, packing, odd, temper, window, dest, tails, near, hidden, far, w_qkv, w_out, gain
):
    rows, channels = hidden.shape
    rim = rows // 4
    tiles = rows // TILE
    seen = rows + 2 * rim
    projected = run_project(layer, hidden, w_qkv)
    shape = (packing, 2 * rows // packing + 8, channels) if packing else (rows, channels)
    return pl.pallas_call(
        functools.partial(sublayer_kernel, layer, packing),
        out_shape=jax.ShapeDtypeStruct(shape, jnp.bfloat16),
        in_specs=[smem] * 3 + [vmem] * 13,
        out_specs=vmem,
        scratch_shapes=[
            pltpu.SMEM((2, tiles), jnp.int32),
            pltpu.VMEM((seen // TILE, TILE), jnp.int32),
            pltpu.VMEM((seen, TILE), jnp.int32),
            pltpu.VMEM((seen, channels), jnp.bfloat16),
            pltpu.VMEM((channels, seen), jnp.bfloat16),
            pltpu.VMEM((tiles, channels, TILE), jnp.float32),
            pltpu.VMEM((rows, channels), jnp.bfloat16),
        ],
        compiler_params=pltpu.CompilerParams(vmem_limit_bytes=vmem_limit),
        cost_estimate=pl.CostEstimate(
            flops=8 * 10**9, bytes_accessed=4 * 10**6, transcendentals=8 * 10**6
        ),
        name="sublayer",
    )(
        odd, temper, window, dest.reshape(tiles, TILE), window.reshape(tiles, TILE), *tails, near,
        hidden, far, *projected, w_qkv, w_out, gain,
    )


def place_kernel(odd_ref, arrived_ref, moved_ref, near_ref, far_ref):
    rows = moved_ref.shape[0]
    rim = near_ref.shape[0]
    devices, padded, channels = arrived_ref.shape
    capacity = padded - 8
    slots = []
    for i in range(devices):
        line = arrived_ref[i, capacity:].astype(jnp.float32)
        value = line[0:1, :capacity] * 32.0 + line[0:1, TILE : TILE + capacity] - 32.0
        slots.append(value.astype(jnp.int32))
    arrived = jnp.concatenate([arrived_ref[i, :capacity] for i in range(devices)], axis=0)
    chunk = min(256, rows)
    for start in range(0, rows, chunk):
        index = lax.broadcasted_iota(jnp.int32, (chunk, capacity), 0) + start
        hits = jnp.concatenate([one_hot(index == slots[i]) for i in range(devices)], axis=1)
        moved_ref[start : start + chunk] = dot(hits, arrived).astype(jnp.bfloat16)
    for out_ref, at_end in ((near_ref, 1 - odd_ref[0]), (far_ref, odd_ref[0])):
        out_ref[...] = moved_ref[pl.ds(pl.multiple_of(at_end * (rows - rim), TILE), rim)]


def run_place(odd, arrived, rows):
    channels = arrived.shape[2]
    edge = jax.ShapeDtypeStruct((rows // 4, channels), jnp.bfloat16)
    return pl.pallas_call(
        place_kernel,
        out_shape=(jax.ShapeDtypeStruct((rows, channels), jnp.bfloat16), edge, edge),
        in_specs=[smem, vmem],
        out_specs=(vmem, vmem, vmem),
        compiler_params=pltpu.CompilerParams(vmem_limit_bytes=vmem_limit),
        cost_estimate=pl.CostEstimate(
            flops=10**9, bytes_accessed=2 * 10**6, transcendentals=0
        ),
        name="place",
    )(odd, arrived)


def exchange(near, far):
    count = lax.axis_size("wide")
    inner = [(i, i + 1) for i in range(0, count - 1, 2)]
    outer = [(i, i + 1) for i in range(1, count - 1, 2)]
    far = lax.ppermute(far, "wide", outer + [(b, a) for a, b in outer])
    near = lax.ppermute(near, "wide", inner + [(b, a) for a, b in inner])
    return near, far


def body(voxels, regular_window, shifted_window, dest, w_qkv, w_out, gain, temper):
    rows, channels = voxels.shape
    devices = lax.axis_size("wide")
    odd = (lax.axis_index("wide").astype(jnp.int32) % 2).reshape(1)
    tails = exchange(*run_edges(odd, voxels, regular_window, shifted_window))
    outgoing = run_sublayer(
        0, devices, odd, temper, regular_window, dest, tails, tails[0], voxels, tails[1], w_qkv,
        w_out, gain,
    )
    arrived = lax.all_to_all(outgoing, "wide", split_axis=0, concat_axis=0, tiled=True)
    moved, near, far = run_place(odd, arrived, rows)
    near, far = exchange(near, far)
    return run_sublayer(
        1, 0, odd, temper, shifted_window, dest, tails, near, moved, far, w_qkv, w_out, gain
    )


def solution(mesh):
    in_specs = (
        P(("parts", "wide"), None),
        P(("parts", "wide")),
        P(("parts", "wide")),
        P(("parts", "wide")),
        P(),
        P(),
        P(),
        P(),
    )
    out_specs = P(("parts", "wide"), None)
    return jax.shard_map(body, mesh=mesh, in_specs=in_specs, out_specs=out_specs, check_vma=False)
```

```python
import functools
import math

import jax
import jax.numpy as jnp
from jax import lax
from jax.experimental import pallas as pl
from jax.experimental.pallas import tpu as pltpu
from jax.sharding import PartitionSpec as P

HEADS = 8
TILE = 128
TAIL = 16

epsilon = 1e-05
masked_score = -1e30
fewest = 2.0**-100
no_mark = 1 << 30
vmem_limit = 40 * 1024 * 1024

vmem = pl.BlockSpec(memory_space=pltpu.VMEM)
smem = pl.BlockSpec(memory_space=pltpu.SMEM)


def dot(a, b):
    return jnp.dot(a, b, preferred_element_type=jnp.float32)


def dot_t(a, b):
    return lax.dot_general(a, b, (((1,), (1,)), ((), ())), preferred_element_type=jnp.float32)


def one_hot(hits):
    return jnp.where(hits, 1.0, 0.0).astype(jnp.bfloat16)


def ranks(match):
    rows, columns = match.shape
    before = one_hot(
        lax.broadcasted_iota(jnp.int32, (TILE, TILE), 0)
        < lax.broadcasted_iota(jnp.int32, (TILE, TILE), 1)
    )
    carry = jnp.zeros((rows, 1), jnp.float32)
    pieces = []
    for start in range(0, columns, TILE):
        piece = match[:, start : start + TILE]
        pieces.append(dot(piece.astype(jnp.bfloat16), before) + carry)
        carry = carry + jnp.sum(piece, axis=1, keepdims=True)
    return jnp.concatenate(pieces, axis=1)


def project_kernel(layer, hidden_ref, w_qkv_ref, query_ref, key_ref, value_ref):
    rows, channels = hidden_ref.shape
    chunk = min(256, rows)
    w_query = jnp.transpose(w_qkv_ref[layer, :, :channels])
    w_value = jnp.transpose(w_qkv_ref[layer, :, 2 * channels :])
    w_both = jnp.concatenate([w_query, w_value], axis=0)
    for start in range(0, rows, chunk):
        here = slice(start, start + chunk)
        source = hidden_ref[here]
        key_ref[here] = dot(source, w_qkv_ref[layer, :, channels : 2 * channels]).astype(
            jnp.bfloat16
        )
        both = dot_t(w_both, source).astype(jnp.bfloat16)
        query_ref[:, here] = both[:channels]
        value_ref[:, here] = both[channels:]


def run_project(layer, hidden, w_qkv):
    rows, channels = hidden.shape
    return pl.pallas_call(
        functools.partial(project_kernel, layer),
        out_shape=(
            jax.ShapeDtypeStruct((channels, rows), jnp.bfloat16),
            jax.ShapeDtypeStruct((rows, channels), jnp.bfloat16),
            jax.ShapeDtypeStruct((channels, rows), jnp.bfloat16),
        ),
        in_specs=[vmem, vmem],
        out_specs=(vmem, vmem, vmem),
        compiler_params=pltpu.CompilerParams(vmem_limit_bytes=vmem_limit),
        cost_estimate=pl.CostEstimate(
            flops=6 * rows * channels * channels, bytes_accessed=3 * 10**6, transcendentals=0
        ),
        name="project",
    )(hidden, w_qkv)


def bound_scores(scales, query_ref, key_ref, bound_ref):
    channels = query_ref.shape[0]
    head_dim = channels // HEADS
    column = lax.broadcasted_iota(jnp.int32, (channels, TILE), 0)
    first = lax.broadcasted_iota(jnp.int32, (channels, TILE), 1) * head_dim
    heads = one_hot((column >= first) & (column < first + head_dim))
    norm = jnp.zeros((1, TILE), jnp.float32)
    for start in range(0, key_ref.shape[0], 2 * TILE):
        keys = key_ref[start : start + 2 * TILE].astype(jnp.float32)
        lengths = dot((keys * keys).astype(jnp.bfloat16), heads)
        norm = jnp.maximum(norm, jnp.max(lengths, axis=0, keepdims=True))
    lane = lax.broadcasted_iota(jnp.int32, (1, TILE), 1)
    for j in range(HEADS):
        query = query_ref[j * head_dim : (j + 1) * head_dim].astype(jnp.float32)
        length = jnp.sum(query * query, axis=0, keepdims=True)
        longest = jnp.sum(jnp.where(lane == j, norm, 0.0), axis=1, keepdims=True)
        bound_ref[j : j + 1] = jnp.sqrt(length * longest) * (scales[j] * -1.01)


def attend_tile(
    number, span_ref, scales, marks_ref, column_ref, bound_ref, query_ref, key_ref, value_ref,
    attended_ref, least_ref, rim,
):
    channels = query_ref.shape[0]
    head_dim = channels // HEADS
    per_group = TILE // head_dim
    here = pl.ds(pl.multiple_of(number * TILE, TILE), TILE)
    most = 1 + 2 * (rim // TILE)
    blank = jnp.zeros((head_dim, TILE), jnp.bfloat16)
    exact = least_ref is None

    def variant(low, tiles):
        span = pl.ds(pl.multiple_of(low * TILE, TILE), tiles * TILE)
        own = marks_ref[pl.ds(number + rim // TILE, 1), :]
        bias = jnp.where(column_ref[span, :] == own, 0.0, masked_score)
        parts = []
        for j in range(HEADS):
            group = j // per_group
            column = [blank] * per_group
            column[j % per_group] = query_ref[j * head_dim : (j + 1) * head_dim, here]
            keys = key_ref[span, group * TILE : (group + 1) * TILE]
            parts.append(dot(keys, jnp.concatenate(column, axis=0)))
        least = None
        for j in range(HEADS):
            if exact:
                part = parts[j] * scales[j] + bias
                part = jnp.exp2(part - jnp.max(part, axis=0, keepdims=True))
            else:
                part = jnp.exp2(parts[j] * scales[j] + (bias + bound_ref[j : j + 1, here]))
            total = jnp.sum(part, axis=0, keepdims=True)
            least = total if j == 0 else jnp.minimum(least, total)
            parts[j] = (part * (1.0 / total)).astype(jnp.bfloat16)
        for j in range(HEADS):
            begin = j * head_dim
            mixed = dot(value_ref[begin : begin + head_dim, span], parts[j])
            attended_ref[pl.ds(number, 1), begin : begin + head_dim] = mixed[None]
        if not exact:
            least_ref[pl.ds(number, 1), :] = least

    low = span_ref[0, number]
    if exact:
        variant(jnp.minimum(low, key_ref.shape[0] // TILE - most), most)
        return
    for tiles in range(2, most + 1):
        pl.when(jnp.maximum(span_ref[1, number], 2) == tiles)(
            functools.partial(variant, low, tiles)
        )


def mark_place(layer, digit, start, rim, channels):
    place = (2 * layer + digit) * rim + start
    return place // channels, place % channels


def halo_marks(tail, layer, rim):
    found = []
    for start in range(0, rim, TILE):
        digits = []
        for digit in range(2):
            line, lane = mark_place(layer, digit, start, rim, tail.shape[1])
            digits.append(tail[line : line + 1, lane : lane + TILE])
        found.append((digits[0] * 256.0 + digits[1]).astype(jnp.int32))
    return found


def tail_of(windows_refs, first_tile, rim, channels):
    which = lax.broadcasted_iota(jnp.int32, (TAIL, TILE), 0)
    columns = [jnp.zeros((TAIL, TILE), jnp.float32) for _ in range(channels // TILE)]
    for layer, window_ref in enumerate(windows_refs):
        for start in range(0, rim, TILE):
            mark = window_ref[pl.ds(first_tile + start // TILE, 1), :] + 1
            for digit, value in enumerate((mark // 256, mark % 256)):
                line, lane = mark_place(layer, digit, start, rim, channels)
                column = columns[lane // TILE]
                columns[lane // TILE] = jnp.where(which == line, value.astype(jnp.float32), column)
    return jnp.concatenate(columns, axis=1).astype(jnp.bfloat16)


def edges_kernel(odd_ref, hidden_ref, regular_ref, shifted_ref, near_ref, far_ref):
    rows, channels = hidden_ref.shape
    rim = rows // 4
    for out_ref, at_end in ((near_ref, 1 - odd_ref[0]), (far_ref, odd_ref[0])):
        start = pl.multiple_of(at_end * (rows - rim), TILE)
        out_ref[:rim] = hidden_ref[pl.ds(start, rim)]
        out_ref[rim:] = tail_of(
            (regular_ref, shifted_ref), at_end * ((rows - rim) // TILE), rim, channels
        )


def run_edges(odd, hidden, regular, shifted):
    rows, channels = hidden.shape
    shape = jax.ShapeDtypeStruct((rows // 4 + TAIL, channels), jnp.bfloat16)
    return pl.pallas_call(
        edges_kernel,
        out_shape=(shape, shape),
        in_specs=[smem, vmem, vmem, vmem],
        out_specs=(vmem, vmem),
        name="edges",
    )(odd, hidden, regular.reshape(-1, TILE), shifted.reshape(-1, TILE))


def sublayer_kernel(
    layer, packing, odd_ref, temper_ref, window_ref, dest_ref, marks_own_ref, near_tail_ref,
    far_tail_ref, near_ref, hidden_ref, far_ref, query_ref, key_own_ref, value_own_ref, w_qkv_ref, w_out_ref,
    gain_ref, out_ref, span_ref, marks_ref, column_ref, key_ref, value_ref, bound_ref, attended_ref, first_ref,
    least_ref,
):
    rows, channels = hidden_ref.shape
    rim = rows // 4
    rim_tiles, own_tiles = rim // TILE, rows // TILE
    factor = (1.0 / math.sqrt(channels // HEADS)) * math.log2(math.e)
    scales = [temper_ref[layer, j] * factor for j in range(HEADS)]

    odd = odd_ref[0]
    near_tail = near_tail_ref[rim : rim + TAIL].astype(jnp.float32)
    far_tail = far_tail_ref[rim : rim + TAIL].astype(jnp.float32)
    is_odd = jnp.full(near_tail.shape, odd, jnp.int32) == 1
    low_marks = halo_marks(jnp.where(is_odd, near_tail, far_tail), layer, rim)
    high_marks = halo_marks(jnp.where(is_odd, far_tail, near_tail), layer, rim)
    high_marks = [jnp.where(m == 0, no_mark, m) for m in high_marks]
    for i in range(rim_tiles):
        marks_ref[i : i + 1] = low_marks[i]
        marks_ref[rim_tiles + own_tiles + i : rim_tiles + own_tiles + i + 1] = high_marks[i]
    marks_ref[rim_tiles : rim_tiles + own_tiles] = marks_own_ref[...] + 1
    lasts = [jnp.max(m) for m in low_marks]
    firsts = [jnp.min(m) for m in high_marks]
    own_first = [window_ref[i * TILE] + 1 for i in range(own_tiles)]
    own_last = [window_ref[(i + 1) * TILE - 1] + 1 for i in range(own_tiles)]
    for t in range(own_tiles):
        begin = jnp.int32(0)
        for mark in lasts + own_last[:t]:
            begin += (mark < own_first[t]).astype(jnp.int32)
        end = jnp.int32(rim_tiles + t + 1)
        for mark in own_first[t + 1 :] + firsts:
            end += (mark <= own_last[t]).astype(jnp.int32)
        span_ref[0, t] = begin
        span_ref[1, t] = end - begin
    for i in range(2 * rim_tiles + own_tiles):
        column_ref[i * TILE : (i + 1) * TILE] = jnp.transpose(
            jnp.broadcast_to(marks_ref[i : i + 1, :], (TILE, TILE))
        )

    w_value = jnp.transpose(w_qkv_ref[layer, :, 2 * channels :])
    key_ref[rim : rim + rows] = key_own_ref[...]
    value_ref[:, rim : rim + rows] = value_own_ref[...]
    for source, at_end in ((near_ref, 1 - odd), (far_ref, odd)):
        source = source[:rim]
        there = pl.ds(pl.multiple_of(at_end * (rim + rows), TILE), rim)
        key_ref[there] = dot(source, w_qkv_ref[layer, :, channels : 2 * channels]).astype(
            jnp.bfloat16
        )
        value_ref[:, there] = dot_t(w_value, source).astype(jnp.bfloat16)

    bound_scores(scales, query_ref, key_ref, bound_ref)
    refs = (span_ref, scales, marks_ref, column_ref, bound_ref, query_ref, key_ref, value_ref)

    def one_tile(number, nothing):
        attend_tile(number, *refs, attended_ref, least_ref, rim)
        return nothing

    lax.fori_loop(0, own_tiles, one_tile, 0)

    @pl.when(jnp.logical_not(jnp.min(least_ref[...]) >= fewest))
    def some_again():
        def one_again(number, nothing):
            @pl.when(jnp.logical_not(jnp.min(least_ref[pl.ds(number, 1), :]) >= fewest))
            def again():
                attend_tile(number, *refs, attended_ref, None, rim)

            return nothing

        lax.fori_loop(0, own_tiles, one_again, 0)

    final_ref = first_ref if packing else out_ref
    for number in range(own_tiles):
        here = slice(number * TILE, (number + 1) * TILE)
        attended = jnp.transpose(attended_ref[number]).astype(jnp.bfloat16)
        summed = hidden_ref[here].astype(jnp.float32) + dot(attended, w_out_ref[layer])
        center = jnp.mean(summed, axis=1, keepdims=True)
        summed = summed - center
        spread = jnp.mean(jnp.square(summed), axis=1, keepdims=True)
        scaled = summed * lax.rsqrt(spread + epsilon) * gain_ref[layer : layer + 1]
        final_ref[here] = scaled.astype(jnp.bfloat16)
    if packing:
        pack(packing, dest_ref, first_ref, out_ref)


def pack(devices, dest_ref, first_ref, out_ref):
    rows, channels = first_ref.shape
    capacity = 2 * rows // devices
    dest = jnp.concatenate([dest_ref[i : i + 1] for i in range(rows // TILE)], axis=1)
    target = dest // rows
    match = jnp.where(lax.broadcasted_iota(jnp.int32, (devices, rows), 0) == target, 1.0, 0.0)
    place = jnp.sum(ranks(match) * match, axis=0, keepdims=True).astype(jnp.int32)
    place = place + target * capacity
    slot = dest - target * rows
    which = lax.broadcasted_iota(jnp.int32, (TAIL, rows), 0)
    digits = jnp.where(
        which == 0, slot // 32 + 1, jnp.where(which == 1, slot % 32, 0)
    )
    digits = digits.astype(jnp.float32).astype(jnp.bfloat16)
    together = max(1, 512 // capacity)
    index = lax.broadcasted_iota(jnp.int32, (together * capacity, rows), 0)
    for start in range(0, devices, together):
        hits = one_hot(index == place - start * capacity)
        packed = dot(hits, first_ref[...]).astype(jnp.bfloat16)
        slots = dot_t(digits, hits)
        for i in range(together):
            here = slice(i * capacity, (i + 1) * capacity)
            out_ref[start + i, :capacity] = packed[here]
            mine = slots[:, here]
            if capacity < TILE:
                blank = jnp.zeros((TAIL, TILE - capacity), jnp.float32)
                mine = jnp.concatenate([mine, blank], axis=1)
            extra = jnp.concatenate([mine[0:8], pltpu.roll(mine[0:8], 7, 0)], axis=1)
            out_ref[start + i, capacity:] = extra.astype(jnp.bfloat16)


def run_sublayer(
    layer, packing, odd, temper, window, dest, tails, near, hidden, far, w_qkv, w_out, gain
):
    rows, channels = hidden.shape
    rim = rows // 4
    tiles = rows // TILE
    seen = rows + 2 * rim
    projected = run_project(layer, hidden, w_qkv)
    shape = (packing, 2 * rows // packing + 8, channels) if packing else (rows, channels)
    return pl.pallas_call(
        functools.partial(sublayer_kernel, layer, packing),
        out_shape=jax.ShapeDtypeStruct(shape, jnp.bfloat16),
        in_specs=[smem] * 3 + [vmem] * 13,
        out_specs=vmem,
        scratch_shapes=[
            pltpu.SMEM((2, tiles), jnp.int32),
            pltpu.VMEM((seen // TILE, TILE), jnp.int32),
            pltpu.VMEM((seen, TILE), jnp.int32),
            pltpu.VMEM((seen, channels), jnp.bfloat16),
            pltpu.VMEM((channels, seen), jnp.bfloat16),
            pltpu.VMEM((HEADS, rows), jnp.float32),
            pltpu.VMEM((tiles, channels, TILE), jnp.float32),
            pltpu.VMEM((rows, channels), jnp.bfloat16),
            pltpu.VMEM((tiles, TILE), jnp.float32),
        ],
        compiler_params=pltpu.CompilerParams(vmem_limit_bytes=vmem_limit),
        cost_estimate=pl.CostEstimate(
            flops=8 * 10**9, bytes_accessed=4 * 10**6, transcendentals=8 * 10**6
        ),
        name="sublayer",
    )(
        odd, temper, window, dest.reshape(tiles, TILE), window.reshape(tiles, TILE), *tails, near,
        hidden, far, *projected, w_qkv, w_out, gain,
    )


def place_kernel(odd_ref, arrived_ref, moved_ref, near_ref, far_ref):
    rows = moved_ref.shape[0]
    rim = near_ref.shape[0]
    devices, padded, channels = arrived_ref.shape
    capacity = padded - 8
    slots = []
    for i in range(devices):
        line = arrived_ref[i, capacity:].astype(jnp.float32)
        value = line[0:1, :capacity] * 32.0 + line[0:1, TILE : TILE + capacity] - 32.0
        slots.append(value.astype(jnp.int32))
    arrived = jnp.concatenate([arrived_ref[i, :capacity] for i in range(devices)], axis=0)
    chunk = min(256, rows)
    for start in range(0, rows, chunk):
        index = lax.broadcasted_iota(jnp.int32, (chunk, capacity), 0) + start
        hits = jnp.concatenate([one_hot(index == slots[i]) for i in range(devices)], axis=1)
        moved_ref[start : start + chunk] = dot(hits, arrived).astype(jnp.bfloat16)
    for out_ref, at_end in ((near_ref, 1 - odd_ref[0]), (far_ref, odd_ref[0])):
        out_ref[...] = moved_ref[pl.ds(pl.multiple_of(at_end * (rows - rim), TILE), rim)]


def run_place(odd, arrived, rows):
    channels = arrived.shape[2]
    edge = jax.ShapeDtypeStruct((rows // 4, channels), jnp.bfloat16)
    return pl.pallas_call(
        place_kernel,
        out_shape=(jax.ShapeDtypeStruct((rows, channels), jnp.bfloat16), edge, edge),
        in_specs=[smem, vmem],
        out_specs=(vmem, vmem, vmem),
        compiler_params=pltpu.CompilerParams(vmem_limit_bytes=vmem_limit),
        cost_estimate=pl.CostEstimate(
            flops=10**9, bytes_accessed=2 * 10**6, transcendentals=0
        ),
        name="place",
    )(odd, arrived)


def exchange(near, far):
    count = lax.axis_size("wide")
    inner = [(i, i + 1) for i in range(0, count - 1, 2)]
    outer = [(i, i + 1) for i in range(1, count - 1, 2)]
    far = lax.ppermute(far, "wide", outer + [(b, a) for a, b in outer])
    near = lax.ppermute(near, "wide", inner + [(b, a) for a, b in inner])
    return near, far


def body(voxels, regular_window, shifted_window, dest, w_qkv, w_out, gain, temper):
    rows, channels = voxels.shape
    devices = lax.axis_size("wide")
    odd = (lax.axis_index("wide").astype(jnp.int32) % 2).reshape(1)
    tails = exchange(*run_edges(odd, voxels, regular_window, shifted_window))
    outgoing = run_sublayer(
        0, devices, odd, temper, regular_window, dest, tails, tails[0], voxels, tails[1], w_qkv,
        w_out, gain,
    )
    arrived = lax.all_to_all(outgoing, "wide", split_axis=0, concat_axis=0, tiled=True)
    moved, near, far = run_place(odd, arrived, rows)
    near, far = exchange(near, far)
    return run_sublayer(
        1, 0, odd, temper, shifted_window, dest, tails, near, moved, far, w_qkv, w_out, gain
    )


def solution(mesh):
    in_specs = (
        P(("parts", "wide"), None),
        P(("parts", "wide")),
        P(("parts", "wide")),
        P(("parts", "wide")),
        P(),
        P(),
        P(),
        P(),
    )
    out_specs = P(("parts", "wide"), None)
    return jax.shard_map(body, mesh=mesh, in_specs=in_specs, out_specs=out_specs, check_vma=False)
```

```python
import functools
import math

import jax
import jax.numpy as jnp
from jax import lax
from jax.experimental import pallas as pl
from jax.experimental.pallas import tpu as pltpu
from jax.sharding import PartitionSpec as P

HEADS = 8
TILE = 128
TAIL = 16

epsilon = 1e-05
masked_score = -1e30
fewest = 2.0**-100
no_mark = 1 << 30
vmem_limit = 40 * 1024 * 1024

vmem = pl.BlockSpec(memory_space=pltpu.VMEM)
hbm = pl.BlockSpec(memory_space=pltpu.HBM)
smem = pl.BlockSpec(memory_space=pltpu.SMEM)


def dot(a, b):
    return jnp.dot(a, b, preferred_element_type=jnp.float32)


def dot_t(a, b):
    return lax.dot_general(a, b, (((1,), (1,)), ((), ())), preferred_element_type=jnp.float32)


def one_hot(hits):
    return jnp.where(hits, 1.0, 0.0).astype(jnp.bfloat16)


def ranks(match):
    rows, columns = match.shape
    before = one_hot(
        lax.broadcasted_iota(jnp.int32, (TILE, TILE), 0)
        < lax.broadcasted_iota(jnp.int32, (TILE, TILE), 1)
    )
    carry = jnp.zeros((rows, 1), jnp.float32)
    pieces = []
    for start in range(0, columns, TILE):
        piece = match[:, start : start + TILE]
        pieces.append(dot(piece.astype(jnp.bfloat16), before) + carry)
        carry = carry + jnp.sum(piece, axis=1, keepdims=True)
    return jnp.concatenate(pieces, axis=1)


def project(layer, hidden_ref, w_qkv_ref, query_ref, key_ref, value_ref):
    rows, channels = hidden_ref.shape
    chunk = min(256, rows)
    w_query = jnp.transpose(w_qkv_ref[layer, :, :channels])
    w_value = jnp.transpose(w_qkv_ref[layer, :, 2 * channels :])
    w_both = jnp.concatenate([w_query, w_value], axis=0)
    for start in range(0, rows, chunk):
        here = slice(start, start + chunk)
        source = hidden_ref[here]
        key_ref[here] = dot(source, w_qkv_ref[layer, :, channels : 2 * channels]).astype(
            jnp.bfloat16
        )
        both = dot_t(w_both, source).astype(jnp.bfloat16)
        query_ref[:, here] = both[:channels]
        value_ref[:, here] = both[channels:]


def projected_shapes(rows, channels):
    return (
        jax.ShapeDtypeStruct((channels, rows), jnp.bfloat16),
        jax.ShapeDtypeStruct((rows, channels), jnp.bfloat16),
        jax.ShapeDtypeStruct((channels, rows), jnp.bfloat16),
    )


def bound_scores(scales, query_ref, key_ref, bound_ref):
    channels = query_ref.shape[0]
    head_dim = channels // HEADS
    column = lax.broadcasted_iota(jnp.int32, (channels, TILE), 0)
    first = lax.broadcasted_iota(jnp.int32, (channels, TILE), 1) * head_dim
    heads = one_hot((column >= first) & (column < first + head_dim))
    norm = jnp.zeros((1, TILE), jnp.float32)
    for start in range(0, key_ref.shape[0], 2 * TILE):
        keys = key_ref[start : start + 2 * TILE].astype(jnp.float32)
        lengths = dot((keys * keys).astype(jnp.bfloat16), heads)
        norm = jnp.maximum(norm, jnp.max(lengths, axis=0, keepdims=True))
    lane = lax.broadcasted_iota(jnp.int32, (1, TILE), 1)
    for j in range(HEADS):
        query = query_ref[j * head_dim : (j + 1) * head_dim].astype(jnp.float32)
        length = jnp.sum(query * query, axis=0, keepdims=True)
        longest = jnp.sum(jnp.where(lane == j, norm, 0.0), axis=1, keepdims=True)
        bound_ref[j : j + 1] = jnp.sqrt(length * longest) * (scales[j] * -1.01)


def attend_tile(
    number, first_tile, span_ref, scales, marks_own_ref, column_ref, bound_ref, query_ref, key_ref,
    value_ref, attended_ref, least_ref, rim,
):
    channels = query_ref.shape[0]
    head_dim = channels // HEADS
    per_group = TILE // head_dim
    tile = first_tile + number
    here = pl.ds(pl.multiple_of(tile * TILE, TILE), TILE)
    most = 1 + 2 * (rim // TILE)
    blank = jnp.zeros((head_dim, TILE), jnp.bfloat16)
    exact = least_ref is None

    def variant(low, tiles):
        span = pl.ds(pl.multiple_of(low * TILE, TILE), tiles * TILE)
        own = marks_own_ref[pl.ds(tile, 1), :] + 1
        bias = jnp.where(column_ref[span, :] == own, 0.0, masked_score)
        parts = []
        for j in range(HEADS):
            group = j // per_group
            column = [blank] * per_group
            column[j % per_group] = query_ref[j * head_dim : (j + 1) * head_dim, here]
            keys = key_ref[span, group * TILE : (group + 1) * TILE]
            parts.append(dot(keys, jnp.concatenate(column, axis=0)))
        least = None
        for j in range(HEADS):
            if exact:
                part = parts[j] * scales[j] + bias
                part = jnp.exp2(part - jnp.max(part, axis=0, keepdims=True))
            else:
                part = jnp.exp2(parts[j] * scales[j] + (bias + bound_ref[j : j + 1, here]))
            total = jnp.sum(part, axis=0, keepdims=True)
            least = total if j == 0 else jnp.minimum(least, total)
            parts[j] = (part * (1.0 / total)).astype(jnp.bfloat16)
        for j in range(HEADS):
            begin = j * head_dim
            mixed = dot(value_ref[begin : begin + head_dim, span], parts[j])
            attended_ref[pl.ds(number, 1), begin : begin + head_dim] = mixed[None]
        if not exact:
            least_ref[pl.ds(number, 1), :] = least

    low = span_ref[0, number]
    if exact:
        variant(jnp.minimum(low, key_ref.shape[0] // TILE - most), most)
        return
    for tiles in range(2, most + 1):
        pl.when(jnp.maximum(span_ref[1, number], 2) == tiles)(
            functools.partial(variant, low, tiles)
        )


def mark_place(layer, digit, start, rim, channels):
    place = (2 * layer + digit) * rim + start
    return place // channels, place % channels


def halo_marks(tail, layer, rim):
    found = []
    for start in range(0, rim, TILE):
        digits = []
        for digit in range(2):
            line, lane = mark_place(layer, digit, start, rim, tail.shape[1])
            digits.append(tail[line : line + 1, lane : lane + TILE])
        found.append((digits[0] * 256.0 + digits[1]).astype(jnp.int32))
    return found


def tail_of(windows_refs, first_tile, rim, channels):
    which = lax.broadcasted_iota(jnp.int32, (TAIL, TILE), 0)
    columns = [jnp.zeros((TAIL, TILE), jnp.float32) for _ in range(channels // TILE)]
    for layer, window_ref in enumerate(windows_refs):
        for start in range(0, rim, TILE):
            mark = window_ref[pl.ds(first_tile + start // TILE, 1), :] + 1
            for digit, value in enumerate((mark // 256, mark % 256)):
                line, lane = mark_place(layer, digit, start, rim, channels)
                column = columns[lane // TILE]
                columns[lane // TILE] = jnp.where(which == line, value.astype(jnp.float32), column)
    return jnp.concatenate(columns, axis=1).astype(jnp.bfloat16)


def start_kernel(
    odd_ref, hidden_in_ref, regular_in_ref, shifted_in_ref, w_in_ref, near_ref, far_ref, query_ref,
    key_ref, value_ref, hidden_ref, w_qkv_ref, parity_ref, regular_ref, shifted_ref, sems,
):
    rows, channels = hidden_ref.shape
    rim = rows // 4
    copies = [
        pltpu.make_async_copy(hidden_in_ref, hidden_ref, sems.at[0]),
        pltpu.make_async_copy(w_in_ref.at[pl.ds(0, 1)], w_qkv_ref, sems.at[1]),
        pltpu.make_async_copy(regular_in_ref, regular_ref, sems.at[2]),
        pltpu.make_async_copy(shifted_in_ref, shifted_ref, sems.at[3]),
    ]
    for copy in copies:
        copy.start()
    for copy in copies:
        copy.wait()
    odd = odd_ref[0]
    parity_ref[...] = jnp.full(parity_ref.shape, odd, jnp.int32)
    for out_ref, at_end in ((near_ref, 1 - odd), (far_ref, odd)):
        start = pl.multiple_of(at_end * (rows - rim), TILE)
        out_ref[:rim] = hidden_ref[pl.ds(start, rim)]
        out_ref[rim:] = tail_of(
            (regular_ref, shifted_ref), at_end * ((rows - rim) // TILE), rim, channels
        )
    project(0, hidden_ref, w_qkv_ref, query_ref, key_ref, value_ref)


def run_start(odd, hidden, regular, shifted, w_qkv):
    rows, channels = hidden.shape
    edge = pltpu.VMEM((rows // 4 + TAIL, channels), jnp.bfloat16)
    return pl.pallas_call(
        start_kernel,
        out_shape=(
            edge,
            edge,
            *[pltpu.VMEM(x.shape, x.dtype) for x in projected_shapes(rows, channels)],
            pltpu.VMEM(hidden.shape, hidden.dtype),
            pltpu.VMEM((1,) + w_qkv.shape[1:], w_qkv.dtype),
            pltpu.VMEM((8, TILE), jnp.int32),
        ),
        in_specs=[smem] + [hbm] * 4,
        out_specs=(vmem,) * 8,
        scratch_shapes=[
            pltpu.VMEM((rows // TILE, TILE), jnp.int32),
            pltpu.VMEM((rows // TILE, TILE), jnp.int32),
            pltpu.SemaphoreType.DMA((4,)),
        ],

        name="start",
    )(odd, hidden, regular.reshape(-1, TILE), shifted.reshape(-1, TILE), w_qkv)


def attend_kernel(
    layer, far, packing, odd_ref, temper_ref, marks_own_ref, tail_ref, halo_ref,
    hidden_ref, query_ref, key_own_ref, value_own_ref, w_qkv_ref, w_out_ref, gain_ref, *refs,
):
    if far:
        done_ref, dest_ref, *refs = refs
    (
        out_ref, span_ref, marks_ref, column_ref, key_ref, value_ref, bound_ref, attended_ref,
        first_ref, least_ref,
    ) = refs
    rows, channels = hidden_ref.shape
    rim = rows // 4
    rim_tiles, own_tiles = rim // TILE, rows // TILE
    in_view = 2 * rim if far else rows
    odd = jnp.max(odd_ref[...])
    at_end = odd if far else 1 - odd
    own_tile = at_end * ((rows - in_view) // TILE)
    own_at = (1 - at_end) * rim_tiles
    halo_at = at_end * (in_view // TILE)
    count = rim_tiles if far else own_tiles - rim_tiles
    first_tile = at_end * (own_tiles - count)
    factor = (1.0 / math.sqrt(channels // HEADS)) * math.log2(math.e)
    scales = [temper_ref[layer : layer + 1, j : j + 1] * factor for j in range(HEADS)]

    past_end = jnp.max(marks_own_ref[...]) + 2
    halo = halo_marks(tail_ref[rim : rim + TAIL].astype(jnp.float32), layer, rim)
    halo = [jnp.where((m == 0) & (at_end == 1), past_end, m) for m in halo]
    marks_ref[pl.ds(own_at, in_view // TILE), :] = (
        marks_own_ref[pl.ds(own_tile, in_view // TILE), :] + 1
    )
    for i in range(rim_tiles):
        marks_ref[pl.ds(halo_at + i, 1), :] = halo[i]
    begins, ends = [], []
    for i in range(marks_ref.shape[0]):
        marks = marks_ref[i : i + 1]
        begins.append(jnp.min(marks))
        ends.append(jnp.max(marks))
    for number in range(count):
        marks = marks_own_ref[pl.ds(first_tile + number, 1), :] + 1
        lowest, highest = jnp.min(marks), jnp.max(marks)
        begin, end = jnp.int32(0), jnp.int32(0)
        for i in range(len(begins)):
            begin += (ends[i] < lowest).astype(jnp.int32)
            end += (begins[i] <= highest).astype(jnp.int32)
        span_ref[0, number] = begin
        span_ref[1, number] = end - begin
    for i in range(marks_ref.shape[0]):
        column_ref[i * TILE : (i + 1) * TILE] = jnp.transpose(
            jnp.broadcast_to(marks_ref[i : i + 1, :], (TILE, TILE))
        )

    there = pl.ds(pl.multiple_of(own_at * TILE, TILE), in_view)
    own = pl.ds(pl.multiple_of(own_tile * TILE, TILE), in_view)
    key_ref[there] = key_own_ref[own]
    value_ref[:, there] = value_own_ref[:, own]
    there = pl.ds(pl.multiple_of(halo_at * TILE, TILE), rim)
    source = halo_ref[:rim]
    w_value = jnp.transpose(w_qkv_ref[w_qkv_ref.shape[0] - 1, :, 2 * channels :])
    key_ref[there] = dot(source, w_qkv_ref[w_qkv_ref.shape[0] - 1, :, channels : 2 * channels]).astype(jnp.bfloat16)
    value_ref[:, there] = dot_t(w_value, source).astype(jnp.bfloat16)
    bound_scores(scales, query_ref, key_ref, bound_ref)
    shared = (span_ref, scales, marks_own_ref, column_ref, bound_ref, query_ref, key_ref, value_ref)

    def one_tile(number, nothing):
        attend_tile(number, first_tile, *shared, attended_ref, least_ref, rim)
        return nothing

    lax.fori_loop(0, count, one_tile, 0)

    @pl.when(jnp.logical_not(jnp.min(least_ref[...]) >= fewest))
    def some_again():
        def one_again(number, nothing):
            @pl.when(jnp.logical_not(jnp.min(least_ref[pl.ds(number, 1), :]) >= fewest))
            def again():
                attend_tile(number, first_tile, *shared, attended_ref, None, rim)

            return nothing

        lax.fori_loop(0, count, one_again, 0)

    final_ref = first_ref if packing else out_ref
    if far:
        other_tile = (1 - at_end) * rim_tiles
        other = pl.ds(pl.multiple_of(other_tile * TILE, TILE), rows - rim)
        final_ref[other] = done_ref[other]
    for number in range(count):
        here = pl.ds(pl.multiple_of((first_tile + number) * TILE, TILE), TILE)
        attended = jnp.transpose(attended_ref[number]).astype(jnp.bfloat16)
        summed = hidden_ref[here].astype(jnp.float32) + dot(attended, w_out_ref[layer])
        center = jnp.mean(summed, axis=1, keepdims=True)
        summed = summed - center
        spread = jnp.mean(jnp.square(summed), axis=1, keepdims=True)
        scaled = summed * lax.rsqrt(spread + epsilon) * gain_ref[layer : layer + 1]
        final_ref[here] = scaled.astype(jnp.bfloat16)
    if packing:
        pack(packing, dest_ref, first_ref, out_ref)


def pack(devices, dest_ref, first_ref, out_ref):
    rows, channels = first_ref.shape
    capacity = 2 * rows // devices
    dest = jnp.concatenate([dest_ref[i : i + 1] for i in range(rows // TILE)], axis=1)
    target = dest // rows
    match = jnp.where(lax.broadcasted_iota(jnp.int32, (devices, rows), 0) == target, 1.0, 0.0)
    place = jnp.sum(ranks(match) * match, axis=0, keepdims=True).astype(jnp.int32)
    place = place + target * capacity
    slot = dest - target * rows
    which = lax.broadcasted_iota(jnp.int32, (TAIL, rows), 0)
    digits = jnp.where(
        which == 0, slot // 32 + 1, jnp.where(which == 1, slot % 32, 0)
    )
    digits = digits.astype(jnp.float32).astype(jnp.bfloat16)
    together = max(1, 512 // capacity)
    index = lax.broadcasted_iota(jnp.int32, (together * capacity, rows), 0)
    for start in range(0, devices, together):
        hits = one_hot(index == place - start * capacity)
        packed = dot(hits, first_ref[...]).astype(jnp.bfloat16)
        slots = dot_t(digits, hits)
        for i in range(together):
            here = slice(i * capacity, (i + 1) * capacity)
            out_ref[start + i, :capacity] = packed[here]
            mine = slots[:, here]
            if capacity < TILE:
                blank = jnp.zeros((TAIL, TILE - capacity), jnp.float32)
                mine = jnp.concatenate([mine, blank], axis=1)
            extra = jnp.concatenate([mine[0:8], pltpu.roll(mine[0:8], 7, 0)], axis=1)
            out_ref[start + i, capacity:] = extra.astype(jnp.bfloat16)


def run_attend(layer, far, packing, operands, more=()):
    rows, channels = operands[5].shape
    rim = rows // 4
    tiles = rows // TILE
    count = rim // TILE if far else tiles - rim // TILE
    view = rim + (2 * rim if far else rows)
    shape = (packing, 2 * rows // packing + 8, channels) if packing else (rows, channels)
    return pl.pallas_call(
        functools.partial(attend_kernel, layer, far, packing),
        out_shape=jax.ShapeDtypeStruct(shape, jnp.bfloat16),
        in_specs=[vmem] * (len(operands) + len(more)),
        out_specs=vmem,
        scratch_shapes=[
            pltpu.SMEM((2, count), jnp.int32),
            pltpu.VMEM((view // TILE, TILE), jnp.int32),
            pltpu.VMEM((view, TILE), jnp.int32),
            pltpu.VMEM((view, channels), jnp.bfloat16),
            pltpu.VMEM((channels, view), jnp.bfloat16),
            pltpu.VMEM((HEADS, rows), jnp.float32),
            pltpu.VMEM((count, channels, TILE), jnp.float32),
            pltpu.VMEM((rows, channels), jnp.bfloat16),
            pltpu.VMEM((count, TILE), jnp.float32),
        ],
        compiler_params=pltpu.CompilerParams(vmem_limit_bytes=vmem_limit),
        cost_estimate=pl.CostEstimate(
            flops=10**9 * count, bytes_accessed=4 * 10**6, transcendentals=10**6 * count
        ),
        name="far" if far else "near",
    )(*operands, *more)


def run_sublayer(layer, packing, odd, temper, window, dest, tails, near, far, hidden, projected, weights):
    marks = window.reshape(-1, TILE)

    def operands(tail, halo):
        return (odd, temper, marks, tail, halo, hidden, *projected, *weights)

    done = run_attend(layer, False, 0, operands(tails[0], near))
    return run_attend(
        layer, True, packing, operands(tails[1], far), (done, dest.reshape(-1, TILE))
    )


def place_kernel(odd_ref, arrived_ref, w_qkv_ref, moved_ref, near_ref, far_ref, *projected_refs):
    odd = jnp.max(odd_ref[...])
    rows = moved_ref.shape[0]
    rim = near_ref.shape[0]
    devices, padded, channels = arrived_ref.shape
    capacity = padded - 8
    slots = []
    for i in range(devices):
        line = arrived_ref[i, capacity:].astype(jnp.float32)
        value = line[0:1, :capacity] * 32.0 + line[0:1, TILE : TILE + capacity] - 32.0
        slots.append(value.astype(jnp.int32))
    arrived = jnp.concatenate([arrived_ref[i, :capacity] for i in range(devices)], axis=0)
    chunk = min(256, rows)
    for start in range(0, rows, chunk):
        index = lax.broadcasted_iota(jnp.int32, (chunk, capacity), 0) + start
        hits = jnp.concatenate([one_hot(index == slots[i]) for i in range(devices)], axis=1)
        moved_ref[start : start + chunk] = dot(hits, arrived).astype(jnp.bfloat16)
    project(1, moved_ref, w_qkv_ref, *projected_refs)
    for out_ref, at_end in ((near_ref, 1 - odd), (far_ref, odd)):
        out_ref[...] = moved_ref[pl.ds(pl.multiple_of(at_end * (rows - rim), TILE), rim)]


def run_place(odd, arrived, rows, w_qkv):
    channels = arrived.shape[2]
    edge = jax.ShapeDtypeStruct((rows // 4, channels), jnp.bfloat16)
    moved = jax.ShapeDtypeStruct((rows, channels), jnp.bfloat16)
    return pl.pallas_call(
        place_kernel,
        out_shape=(moved, edge, edge, *projected_shapes(rows, channels)),
        in_specs=[vmem] * 3,
        out_specs=(vmem,) * 6,
        compiler_params=pltpu.CompilerParams(vmem_limit_bytes=vmem_limit),
        cost_estimate=pl.CostEstimate(
            flops=10**9, bytes_accessed=2 * 10**6, transcendentals=0
        ),
        name="place",
    )(odd, arrived, w_qkv)


def exchange(near, far):
    count = lax.axis_size("wide")
    inner = [(i, i + 1) for i in range(0, count - 1, 2)]
    outer = [(i, i + 1) for i in range(1, count - 1, 2)]
    far = lax.ppermute(far, "wide", outer + [(b, a) for a, b in outer])
    near = lax.ppermute(near, "wide", inner + [(b, a) for a, b in inner])
    return near, far


def body(voxels, regular_window, shifted_window, dest, w_qkv, w_out, gain, temper):
    rows, channels = voxels.shape
    devices = lax.axis_size("wide")
    odd = lax.axis_index("wide").astype(jnp.int32) % 2
    near, far, *projected, hidden, w_first, odd = run_start(
        odd.reshape(1), voxels, regular_window, shifted_window, w_qkv
    )
    tails = exchange(near, far)
    outgoing = run_sublayer(
        0, devices, odd, temper, regular_window, dest, tails, *tails, hidden, projected,
        (w_first, w_out, gain),
    )
    arrived = lax.all_to_all(outgoing, "wide", split_axis=0, concat_axis=0, tiled=True)
    moved, near, far, *projected = run_place(odd, arrived, rows, w_qkv)
    near, far = exchange(near, far)
    return run_sublayer(
        1, 0, odd, temper, shifted_window, dest, tails, near, far, moved, projected,
        (w_qkv, w_out, gain),
    )


def solution(mesh):
    in_specs = (
        P(("parts", "wide"), None),
        P(("parts", "wide")),
        P(("parts", "wide")),
        P(("parts", "wide")),
        P(),
        P(),
        P(),
        P(),
    )
    out_specs = P(("parts", "wide"), None)
    return jax.shard_map(body, mesh=mesh, in_specs=in_specs, out_specs=out_specs, check_vma=False)
```

```python
import functools
import math

import jax
import jax.numpy as jnp
from jax import lax
from jax.experimental import pallas as pl
from jax.experimental.pallas import tpu as pltpu
from jax.sharding import PartitionSpec as P

HEADS = 8
TILE = 128
TAIL = 16

epsilon = 1e-05
masked_score = -1e30
fewest = 2.0**-100
no_mark = 1 << 30
vmem_limit = 40 * 1024 * 1024

vmem = pl.BlockSpec(memory_space=pltpu.VMEM)
hbm = pl.BlockSpec(memory_space=pltpu.HBM)
smem = pl.BlockSpec(memory_space=pltpu.SMEM)


def dot(a, b):
    return jnp.dot(a, b, preferred_element_type=jnp.float32)


def dot_t(a, b):
    return lax.dot_general(a, b, (((1,), (1,)), ((), ())), preferred_element_type=jnp.float32)


def one_hot(hits):
    return jnp.where(hits, 1.0, 0.0).astype(jnp.bfloat16)


def ranks(match):
    rows, columns = match.shape
    before = one_hot(
        lax.broadcasted_iota(jnp.int32, (TILE, TILE), 0)
        < lax.broadcasted_iota(jnp.int32, (TILE, TILE), 1)
    )
    carry = jnp.zeros((rows, 1), jnp.float32)
    pieces = []
    for start in range(0, columns, TILE):
        piece = match[:, start : start + TILE]
        pieces.append(dot(piece.astype(jnp.bfloat16), before) + carry)
        carry = carry + jnp.sum(piece, axis=1, keepdims=True)
    return jnp.concatenate(pieces, axis=1)


def project(layer, hidden_ref, w_qkv_ref, query_ref, key_ref, value_ref):
    rows, channels = hidden_ref.shape
    chunk = min(256, rows)
    w_query = jnp.transpose(w_qkv_ref[layer, :, :channels])
    w_value = jnp.transpose(w_qkv_ref[layer, :, 2 * channels :])
    w_both = jnp.concatenate([w_query, w_value], axis=0)
    for start in range(0, rows, chunk):
        here = slice(start, start + chunk)
        source = hidden_ref[here]
        key_ref[here] = dot(source, w_qkv_ref[layer, :, channels : 2 * channels]).astype(
            jnp.bfloat16
        )
        both = dot_t(w_both, source).astype(jnp.bfloat16)
        query_ref[:, here] = both[:channels]
        value_ref[:, here] = both[channels:]


def projected_shapes(rows, channels):
    return (
        jax.ShapeDtypeStruct((channels, rows), jnp.bfloat16),
        jax.ShapeDtypeStruct((rows, channels), jnp.bfloat16),
        jax.ShapeDtypeStruct((channels, rows), jnp.bfloat16),
    )


def bound_scores(scales, query_ref, key_ref, bound_ref, wanted):
    channels = query_ref.shape[0]
    head_dim = channels // HEADS
    column = lax.broadcasted_iota(jnp.int32, (channels, TILE), 0)
    first = lax.broadcasted_iota(jnp.int32, (channels, TILE), 1) * head_dim
    heads = one_hot((column >= first) & (column < first + head_dim))
    norm = jnp.zeros((1, TILE), jnp.float32)
    for start in range(0, key_ref.shape[0], 2 * TILE):
        keys = key_ref[start : start + 2 * TILE].astype(jnp.float32)
        lengths = dot((keys * keys).astype(jnp.bfloat16), heads)
        norm = jnp.maximum(norm, jnp.max(lengths, axis=0, keepdims=True))
    lane = lax.broadcasted_iota(jnp.int32, (1, TILE), 1)
    for j in range(HEADS):
        query = query_ref[j * head_dim : (j + 1) * head_dim, wanted].astype(jnp.float32)
        length = jnp.sum(query * query, axis=0, keepdims=True)
        longest = jnp.sum(jnp.where(lane == j, norm, 0.0), axis=1, keepdims=True)
        bound_ref[j : j + 1, wanted] = jnp.sqrt(length * longest) * (scales[j] * -1.01)


def attend_tile(
    number, first_tile, span_ref, scales, marks_own_ref, column_ref, bound_ref, query_ref, key_ref,
    value_ref, attended_ref, least_ref, rim,
):
    channels = query_ref.shape[0]
    head_dim = channels // HEADS
    per_group = TILE // head_dim
    tile = first_tile + number
    here = pl.ds(pl.multiple_of(tile * TILE, TILE), TILE)
    most = 1 + 2 * (rim // TILE)
    blank = jnp.zeros((head_dim, TILE), jnp.bfloat16)
    exact = least_ref is None

    def variant(low, tiles):
        span = pl.ds(pl.multiple_of(low * TILE, TILE), tiles * TILE)
        own = marks_own_ref[pl.ds(tile, 1), :] + 1
        bias = jnp.where(column_ref[span, :] == own, 0.0, masked_score)
        parts = []
        for j in range(HEADS):
            group = j // per_group
            column = [blank] * per_group
            column[j % per_group] = query_ref[j * head_dim : (j + 1) * head_dim, here]
            keys = key_ref[span, group * TILE : (group + 1) * TILE]
            parts.append(dot(keys, jnp.concatenate(column, axis=0)))
        least = None
        for j in range(HEADS):
            if exact:
                part = parts[j] * scales[j] + bias
                part = jnp.exp2(part - jnp.max(part, axis=0, keepdims=True))
            else:
                part = jnp.exp2(parts[j] * scales[j] + (bias + bound_ref[j : j + 1, here]))
            total = jnp.sum(part, axis=0, keepdims=True)
            least = total if j == 0 else jnp.minimum(least, total)
            parts[j] = (part * (1.0 / total)).astype(jnp.bfloat16)
        for j in range(HEADS):
            begin = j * head_dim
            mixed = dot(value_ref[begin : begin + head_dim, span], parts[j])
            attended_ref[pl.ds(number, 1), begin : begin + head_dim] = mixed[None]
        if not exact:
            least_ref[pl.ds(number, 1), :] = least

    low = span_ref[0, number]
    if exact:
        variant(jnp.minimum(low, key_ref.shape[0] // TILE - most), most)
        return
    for tiles in range(2, most + 1):
        pl.when(jnp.maximum(span_ref[1, number], 2) == tiles)(
            functools.partial(variant, low, tiles)
        )


def mark_place(layer, digit, start, rim, channels):
    place = (2 * layer + digit) * rim + start
    return place // channels, place % channels


def halo_marks(tail, layer, rim):
    found = []
    for start in range(0, rim, TILE):
        digits = []
        for digit in range(2):
            line, lane = mark_place(layer, digit, start, rim, tail.shape[1])
            digits.append(tail[line : line + 1, lane : lane + TILE])
        found.append((digits[0] * 256.0 + digits[1]).astype(jnp.int32))
    return found


def tail_of(windows_refs, first_tile, rim, channels):
    which = lax.broadcasted_iota(jnp.int32, (TAIL, TILE), 0)
    columns = [jnp.zeros((TAIL, TILE), jnp.float32) for _ in range(channels // TILE)]
    for layer, window_ref in enumerate(windows_refs):
        for start in range(0, rim, TILE):
            mark = window_ref[pl.ds(first_tile + start // TILE, 1), :] + 1
            for digit, value in enumerate((mark // 256, mark % 256)):
                line, lane = mark_place(layer, digit, start, rim, channels)
                column = columns[lane // TILE]
                columns[lane // TILE] = jnp.where(which == line, value.astype(jnp.float32), column)
    return jnp.concatenate(columns, axis=1).astype(jnp.bfloat16)


def start_kernel(
    odd_ref, hidden_in_ref, regular_in_ref, shifted_in_ref, w_in_ref, near_ref, far_ref, query_ref,
    key_ref, value_ref, hidden_ref, w_qkv_ref, parity_ref, regular_ref, shifted_ref, sems,
):
    rows, channels = hidden_ref.shape
    rim = rows // 4
    copies = [
        pltpu.make_async_copy(hidden_in_ref, hidden_ref, sems.at[0]),
        pltpu.make_async_copy(w_in_ref.at[pl.ds(0, 1)], w_qkv_ref, sems.at[1]),
        pltpu.make_async_copy(regular_in_ref, regular_ref, sems.at[2]),
        pltpu.make_async_copy(shifted_in_ref, shifted_ref, sems.at[3]),
    ]
    for copy in copies:
        copy.start()
    for copy in copies:
        copy.wait()
    odd = odd_ref[0]
    parity_ref[...] = jnp.full(parity_ref.shape, odd, jnp.int32)
    for out_ref, at_end in ((near_ref, 1 - odd), (far_ref, odd)):
        start = pl.multiple_of(at_end * (rows - rim), TILE)
        out_ref[:rim] = hidden_ref[pl.ds(start, rim)]
        out_ref[rim:] = tail_of(
            (regular_ref, shifted_ref), at_end * ((rows - rim) // TILE), rim, channels
        )
    project(0, hidden_ref, w_qkv_ref, query_ref, key_ref, value_ref)


def run_start(odd, hidden, regular, shifted, w_qkv):
    rows, channels = hidden.shape
    edge = pltpu.VMEM((rows // 4 + TAIL, channels), jnp.bfloat16)
    return pl.pallas_call(
        start_kernel,
        out_shape=(
            edge,
            edge,
            *[pltpu.VMEM(x.shape, x.dtype) for x in projected_shapes(rows, channels)],
            pltpu.VMEM(hidden.shape, hidden.dtype),
            pltpu.VMEM((1,) + w_qkv.shape[1:], w_qkv.dtype),
            pltpu.VMEM((8, TILE), jnp.int32),
        ),
        in_specs=[smem] + [hbm] * 4,
        out_specs=(vmem,) * 8,
        scratch_shapes=[
            pltpu.VMEM((rows // TILE, TILE), jnp.int32),
            pltpu.VMEM((rows // TILE, TILE), jnp.int32),
            pltpu.SemaphoreType.DMA((4,)),
        ],

        name="start",
    )(odd, hidden, regular.reshape(-1, TILE), shifted.reshape(-1, TILE), w_qkv)


def attend_kernel(
    layer, far, packing, odd_ref, temper_ref, marks_own_ref, tail_ref, halo_ref,
    hidden_ref, query_ref, key_own_ref, value_own_ref, w_qkv_ref, w_out_ref, gain_ref, *refs,
):
    if far:
        done_ref, dest_ref, *refs = refs
    (
        out_ref, span_ref, marks_ref, column_ref, key_ref, value_ref, bound_ref, attended_ref,
        first_ref, least_ref,
    ) = refs
    rows, channels = hidden_ref.shape
    rim = rows // 4
    rim_tiles, own_tiles = rim // TILE, rows // TILE
    in_view = 2 * rim if far else rows
    odd = jnp.max(odd_ref[...])
    at_end = odd if far else 1 - odd
    own_tile = at_end * ((rows - in_view) // TILE)
    own_at = (1 - at_end) * rim_tiles
    halo_at = at_end * (in_view // TILE)
    count = rim_tiles if far else own_tiles - rim_tiles
    first_tile = at_end * (own_tiles - count)
    factor = (1.0 / math.sqrt(channels // HEADS)) * math.log2(math.e)
    scales = [temper_ref[layer : layer + 1, j : j + 1] * factor for j in range(HEADS)]

    past_end = jnp.max(marks_own_ref[...]) + 2
    halo = halo_marks(tail_ref[rim : rim + TAIL].astype(jnp.float32), layer, rim)
    halo = [jnp.where((m == 0) & (at_end == 1), past_end, m) for m in halo]
    marks_ref[pl.ds(own_at, in_view // TILE), :] = (
        marks_own_ref[pl.ds(own_tile, in_view // TILE), :] + 1
    )
    for i in range(rim_tiles):
        marks_ref[pl.ds(halo_at + i, 1), :] = halo[i]
    begins, ends = [], []
    for i in range(marks_ref.shape[0]):
        marks = marks_ref[i : i + 1]
        begins.append(jnp.min(marks))
        ends.append(jnp.max(marks))
    for number in range(count):
        marks = marks_own_ref[pl.ds(first_tile + number, 1), :] + 1
        lowest, highest = jnp.min(marks), jnp.max(marks)
        begin, end = jnp.int32(0), jnp.int32(0)
        for i in range(len(begins)):
            begin += (ends[i] < lowest).astype(jnp.int32)
            end += (begins[i] <= highest).astype(jnp.int32)
        span_ref[0, number] = begin
        span_ref[1, number] = end - begin
    for i in range(marks_ref.shape[0]):
        column_ref[i * TILE : (i + 1) * TILE] = jnp.transpose(
            jnp.broadcast_to(marks_ref[i : i + 1, :], (TILE, TILE))
        )

    there = pl.ds(pl.multiple_of(own_at * TILE, TILE), in_view)
    own = pl.ds(pl.multiple_of(own_tile * TILE, TILE), in_view)
    key_ref[there] = key_own_ref[own]
    value_ref[:, there] = value_own_ref[:, own]
    there = pl.ds(pl.multiple_of(halo_at * TILE, TILE), rim)
    source = halo_ref[:rim]
    w_value = jnp.transpose(w_qkv_ref[w_qkv_ref.shape[0] - 1, :, 2 * channels :])
    key_ref[there] = dot(source, w_qkv_ref[w_qkv_ref.shape[0] - 1, :, channels : 2 * channels]).astype(jnp.bfloat16)
    value_ref[:, there] = dot_t(w_value, source).astype(jnp.bfloat16)
    wanted = pl.ds(pl.multiple_of(first_tile * TILE, TILE), count * TILE)
    bound_scores(scales, query_ref, key_ref, bound_ref, wanted)
    shared = (span_ref, scales, marks_own_ref, column_ref, bound_ref, query_ref, key_ref, value_ref)

    def one_tile(number, nothing):
        attend_tile(number, first_tile, *shared, attended_ref, least_ref, rim)
        return nothing

    lax.fori_loop(0, count, one_tile, 0)

    @pl.when(jnp.logical_not(jnp.min(least_ref[...]) >= fewest))
    def some_again():
        def one_again(number, nothing):
            @pl.when(jnp.logical_not(jnp.min(least_ref[pl.ds(number, 1), :]) >= fewest))
            def again():
                attend_tile(number, first_tile, *shared, attended_ref, None, rim)

            return nothing

        lax.fori_loop(0, count, one_again, 0)

    final_ref = first_ref if packing else out_ref
    if far:
        other_tile = (1 - at_end) * rim_tiles
        other = pl.ds(pl.multiple_of(other_tile * TILE, TILE), rows - rim)
        final_ref[other] = done_ref[other]
    for number in range(count):
        here = pl.ds(pl.multiple_of((first_tile + number) * TILE, TILE), TILE)
        attended = jnp.transpose(attended_ref[number]).astype(jnp.bfloat16)
        summed = hidden_ref[here].astype(jnp.float32) + dot(attended, w_out_ref[layer])
        center = jnp.mean(summed, axis=1, keepdims=True)
        summed = summed - center
        spread = jnp.mean(jnp.square(summed), axis=1, keepdims=True)
        scaled = summed * lax.rsqrt(spread + epsilon) * gain_ref[layer : layer + 1]
        final_ref[here] = scaled.astype(jnp.bfloat16)
    if packing:
        pack(packing, dest_ref, first_ref, out_ref)


def pack(devices, dest_ref, first_ref, out_ref):
    rows, channels = first_ref.shape
    capacity = 2 * rows // devices
    dest = jnp.concatenate([dest_ref[i : i + 1] for i in range(rows // TILE)], axis=1)
    target = dest // rows
    match = jnp.where(lax.broadcasted_iota(jnp.int32, (devices, rows), 0) == target, 1.0, 0.0)
    rank = jnp.sum(ranks(match) * match, axis=0, keepdims=True).astype(jnp.int32)
    slot = (dest - target * rows).astype(jnp.int32)
    digits = [match * (slot // 32 + 1).astype(jnp.float32), match * (slot % 32).astype(jnp.float32)]
    digits = jnp.concatenate(digits, axis=0).astype(jnp.bfloat16)
    at_rank = one_hot(lax.broadcasted_iota(jnp.int32, (capacity, rows), 0) == rank)
    slots = dot_t(digits, at_rank)
    if capacity < TILE:
        blank = jnp.zeros((2 * devices, TILE - capacity), jnp.float32)
        slots = jnp.concatenate([slots, blank], axis=1)
    slots = jnp.concatenate([slots[:devices], slots[devices:]], axis=1)
    for i in range(devices):
        line = jnp.broadcast_to(slots[i : i + 1], (8, channels)).astype(jnp.bfloat16)
        out_ref[i, capacity:] = line
    place = rank + target * capacity
    together = max(1, 512 // capacity)
    index = lax.broadcasted_iota(jnp.int32, (together * capacity, rows), 0)
    for start in range(0, devices, together):
        hits = one_hot(index == place - start * capacity)
        packed = dot(hits, first_ref[...]).astype(jnp.bfloat16)
        for i in range(together):
            out_ref[start + i, :capacity] = packed[i * capacity : (i + 1) * capacity]


def run_attend(layer, far, packing, operands, more=()):
    rows, channels = operands[5].shape
    rim = rows // 4
    tiles = rows // TILE
    count = rim // TILE if far else tiles - rim // TILE
    view = rim + (2 * rim if far else rows)
    shape = (packing, 2 * rows // packing + 8, channels) if packing else (rows, channels)
    return pl.pallas_call(
        functools.partial(attend_kernel, layer, far, packing),
        out_shape=jax.ShapeDtypeStruct(shape, jnp.bfloat16),
        in_specs=[vmem] * (len(operands) + len(more)),
        out_specs=vmem,
        scratch_shapes=[
            pltpu.SMEM((2, count), jnp.int32),
            pltpu.VMEM((view // TILE, TILE), jnp.int32),
            pltpu.VMEM((view, TILE), jnp.int32),
            pltpu.VMEM((view, channels), jnp.bfloat16),
            pltpu.VMEM((channels, view), jnp.bfloat16),
            pltpu.VMEM((HEADS, rows), jnp.float32),
            pltpu.VMEM((count, channels, TILE), jnp.float32),
            pltpu.VMEM((rows, channels), jnp.bfloat16),
            pltpu.VMEM((count, TILE), jnp.float32),
        ],
        compiler_params=pltpu.CompilerParams(vmem_limit_bytes=vmem_limit),
        cost_estimate=pl.CostEstimate(
            flops=10**9 * count, bytes_accessed=4 * 10**6, transcendentals=10**6 * count
        ),
        name="far" if far else "near",
    )(*operands, *more)


def run_sublayer(layer, packing, odd, temper, window, dest, tails, near, far, hidden, projected, weights):
    marks = window.reshape(-1, TILE)

    def operands(tail, halo):
        return (odd, temper, marks, tail, halo, hidden, *projected, *weights)

    done = run_attend(layer, False, 0, operands(tails[0], near))
    return run_attend(
        layer, True, packing, operands(tails[1], far), (done, dest.reshape(-1, TILE))
    )


def place_kernel(odd_ref, arrived_ref, w_qkv_ref, moved_ref, near_ref, far_ref, *projected_refs):
    odd = jnp.max(odd_ref[...])
    rows = moved_ref.shape[0]
    rim = near_ref.shape[0]
    devices, padded, channels = arrived_ref.shape
    capacity = padded - 8
    slots = []
    for i in range(devices):
        line = arrived_ref[i, capacity:].astype(jnp.float32)
        value = line[0:1, :capacity] * 32.0 + line[0:1, TILE : TILE + capacity] - 32.0
        slots.append(value.astype(jnp.int32))
    arrived = jnp.concatenate([arrived_ref[i, :capacity] for i in range(devices)], axis=0)
    chunk = min(256, rows)
    for start in range(0, rows, chunk):
        index = lax.broadcasted_iota(jnp.int32, (chunk, capacity), 0) + start
        hits = jnp.concatenate([one_hot(index == slots[i]) for i in range(devices)], axis=1)
        moved_ref[start : start + chunk] = dot(hits, arrived).astype(jnp.bfloat16)
    project(1, moved_ref, w_qkv_ref, *projected_refs)
    for out_ref, at_end in ((near_ref, 1 - odd), (far_ref, odd)):
        out_ref[...] = moved_ref[pl.ds(pl.multiple_of(at_end * (rows - rim), TILE), rim)]


def run_place(odd, arrived, rows, w_qkv):
    channels = arrived.shape[2]
    edge = jax.ShapeDtypeStruct((rows // 4, channels), jnp.bfloat16)
    moved = jax.ShapeDtypeStruct((rows, channels), jnp.bfloat16)
    return pl.pallas_call(
        place_kernel,
        out_shape=(moved, edge, edge, *projected_shapes(rows, channels)),
        in_specs=[vmem] * 3,
        out_specs=(vmem,) * 6,
        compiler_params=pltpu.CompilerParams(vmem_limit_bytes=vmem_limit),
        cost_estimate=pl.CostEstimate(
            flops=10**9, bytes_accessed=2 * 10**6, transcendentals=0
        ),
        name="place",
    )(odd, arrived, w_qkv)


def exchange(near, far):
    count = lax.axis_size("wide")
    inner = [(i, i + 1) for i in range(0, count - 1, 2)]
    outer = [(i, i + 1) for i in range(1, count - 1, 2)]
    far = lax.ppermute(far, "wide", outer + [(b, a) for a, b in outer])
    near = lax.ppermute(near, "wide", inner + [(b, a) for a, b in inner])
    return near, far


def body(voxels, regular_window, shifted_window, dest, w_qkv, w_out, gain, temper):
    rows, channels = voxels.shape
    devices = lax.axis_size("wide")
    odd = lax.axis_index("wide").astype(jnp.int32) % 2
    near, far, *projected, hidden, w_first, odd = run_start(
        odd.reshape(1), voxels, regular_window, shifted_window, w_qkv
    )
    tails = exchange(near, far)
    outgoing = run_sublayer(
        0, devices, odd, temper, regular_window, dest, tails, *tails, hidden, projected,
        (w_first, w_out, gain),
    )
    arrived = lax.all_to_all(outgoing, "wide", split_axis=0, concat_axis=0, tiled=True)
    moved, near, far, *projected = run_place(odd, arrived, rows, w_qkv)
    near, far = exchange(near, far)
    return run_sublayer(
        1, 0, odd, temper, shifted_window, dest, tails, near, far, moved, projected,
        (w_qkv, w_out, gain),
    )


def solution(mesh):
    in_specs = (
        P(("parts", "wide"), None),
        P(("parts", "wide")),
        P(("parts", "wide")),
        P(("parts", "wide")),
        P(),
        P(),
        P(),
        P(),
    )
    out_specs = P(("parts", "wide"), None)
    return jax.shard_map(body, mesh=mesh, in_specs=in_specs, out_specs=out_specs, check_vma=False)
```

```python
import functools
import math

import jax
import jax.numpy as jnp
from jax import lax
from jax.experimental import pallas as pl
from jax.experimental.pallas import tpu as pltpu
from jax.sharding import PartitionSpec as P

HEADS = 8
TILE = 128
TAIL = 16

epsilon = 1e-05
masked_score = -1e30
fewest = 2.0**-100
no_mark = 1 << 30
vmem_limit = 40 * 1024 * 1024

vmem = pl.BlockSpec(memory_space=pltpu.VMEM)
hbm = pl.BlockSpec(memory_space=pltpu.HBM)
smem = pl.BlockSpec(memory_space=pltpu.SMEM)


def dot(a, b):
    return jnp.dot(a, b, preferred_element_type=jnp.float32)


def dot_t(a, b):
    return lax.dot_general(a, b, (((1,), (1,)), ((), ())), preferred_element_type=jnp.float32)


def one_hot(hits):
    return jnp.where(hits, 1.0, 0.0).astype(jnp.bfloat16)


def ranks(match):
    rows, columns = match.shape
    before = one_hot(
        lax.broadcasted_iota(jnp.int32, (TILE, TILE), 0)
        < lax.broadcasted_iota(jnp.int32, (TILE, TILE), 1)
    )
    carry = jnp.zeros((rows, 1), jnp.float32)
    pieces = []
    for start in range(0, columns, TILE):
        piece = match[:, start : start + TILE]
        pieces.append(dot(piece.astype(jnp.bfloat16), before) + carry)
        carry = carry + jnp.sum(piece, axis=1, keepdims=True)
    return jnp.concatenate(pieces, axis=1)


def project(layer, hidden_ref, w_qkv_ref, query_ref, key_ref, value_ref):
    rows, channels = hidden_ref.shape
    chunk = min(256, rows)
    w_query = jnp.transpose(w_qkv_ref[layer, :, :channels])
    w_value = jnp.transpose(w_qkv_ref[layer, :, 2 * channels :])
    w_both = jnp.concatenate([w_query, w_value], axis=0)
    for start in range(0, rows, chunk):
        here = slice(start, start + chunk)
        source = hidden_ref[here]
        key_ref[here] = dot(source, w_qkv_ref[layer, :, channels : 2 * channels]).astype(
            jnp.bfloat16
        )
        both = dot_t(w_both, source).astype(jnp.bfloat16)
        query_ref[:, here] = both[:channels]
        value_ref[:, here] = both[channels:]


def projected_shapes(rows, channels):
    return (
        jax.ShapeDtypeStruct((channels, rows), jnp.bfloat16),
        jax.ShapeDtypeStruct((rows, channels), jnp.bfloat16),
        jax.ShapeDtypeStruct((channels, rows), jnp.bfloat16),
    )


def bound_scores(scales, query_ref, key_ref, bound_ref, wanted):
    channels = query_ref.shape[0]
    head_dim = channels // HEADS
    column = lax.broadcasted_iota(jnp.int32, (channels, TILE), 0)
    first = lax.broadcasted_iota(jnp.int32, (channels, TILE), 1) * head_dim
    heads = one_hot((column >= first) & (column < first + head_dim))
    norm = jnp.zeros((1, TILE), jnp.float32)
    for start in range(0, key_ref.shape[0], 2 * TILE):
        keys = key_ref[start : start + 2 * TILE].astype(jnp.float32)
        lengths = dot((keys * keys).astype(jnp.bfloat16), heads)
        norm = jnp.maximum(norm, jnp.max(lengths, axis=0, keepdims=True))
    lane = lax.broadcasted_iota(jnp.int32, (1, TILE), 1)
    for j in range(HEADS):
        query = query_ref[j * head_dim : (j + 1) * head_dim, wanted].astype(jnp.float32)
        length = jnp.sum(query * query, axis=0, keepdims=True)
        longest = jnp.sum(jnp.where(lane == j, norm, 0.0), axis=1, keepdims=True)
        bound_ref[j : j + 1, wanted] = jnp.sqrt(length * longest) * (scales[j] * -1.01)


def attend_tile(
    number, first_tile, span_ref, scales, marks_own_ref, column_ref, bound_ref, query_ref, key_ref,
    value_ref, attended_ref, least_ref, rim,
):
    channels = query_ref.shape[0]
    head_dim = channels // HEADS
    per_group = TILE // head_dim
    tile = first_tile + number
    here = pl.ds(pl.multiple_of(tile * TILE, TILE), TILE)
    most = 1 + 2 * (rim // TILE)
    blank = jnp.zeros((head_dim, TILE), jnp.bfloat16)
    exact = least_ref is None

    def variant(low, tiles):
        span = pl.ds(pl.multiple_of(low * TILE, TILE), tiles * TILE)
        own = marks_own_ref[pl.ds(tile, 1), :] + 1
        bias = jnp.where(column_ref[span, :] == own, 0.0, masked_score)
        parts = []
        for j in range(HEADS):
            group = j // per_group
            column = [blank] * per_group
            column[j % per_group] = query_ref[j * head_dim : (j + 1) * head_dim, here]
            keys = key_ref[span, group * TILE : (group + 1) * TILE]
            parts.append(dot(keys, jnp.concatenate(column, axis=0)))
        least = None
        for j in range(HEADS):
            if exact:
                part = parts[j] * scales[j] + bias
                part = jnp.exp2(part - jnp.max(part, axis=0, keepdims=True))
            else:
                part = jnp.exp2(parts[j] * scales[j] + (bias + bound_ref[j : j + 1, here]))
            total = jnp.sum(part, axis=0, keepdims=True)
            least = total if j == 0 else jnp.minimum(least, total)
            parts[j] = (part * (1.0 / total)).astype(jnp.bfloat16)
        for j in range(HEADS):
            begin = j * head_dim
            mixed = dot(value_ref[begin : begin + head_dim, span], parts[j])
            attended_ref[pl.ds(number, 1), begin : begin + head_dim] = mixed[None]
        if not exact:
            least_ref[pl.ds(number, 1), :] = least

    low = span_ref[0, number]
    if exact:
        variant(jnp.minimum(low, key_ref.shape[0] // TILE - most), most)
        return
    for tiles in range(2, most + 1):
        pl.when(jnp.maximum(span_ref[1, number], 2) == tiles)(
            functools.partial(variant, low, tiles)
        )


def mark_place(layer, digit, start, rim, channels):
    place = (2 * layer + digit) * rim + start
    return place // channels, place % channels


def halo_marks(tail, layer, rim):
    found = []
    for start in range(0, rim, TILE):
        digits = []
        for digit in range(2):
            line, lane = mark_place(layer, digit, start, rim, tail.shape[1])
            digits.append(tail[line : line + 1, lane : lane + TILE])
        found.append((digits[0] * 256.0 + digits[1]).astype(jnp.int32))
    return found


def tail_of(windows_refs, first_tile, rim, channels):
    which = lax.broadcasted_iota(jnp.int32, (TAIL, TILE), 0)
    columns = [jnp.zeros((TAIL, TILE), jnp.float32) for _ in range(channels // TILE)]
    for layer, window_ref in enumerate(windows_refs):
        for start in range(0, rim, TILE):
            mark = window_ref[pl.ds(first_tile + start // TILE, 1), :] + 1
            for digit, value in enumerate((mark // 256, mark % 256)):
                line, lane = mark_place(layer, digit, start, rim, channels)
                column = columns[lane // TILE]
                columns[lane // TILE] = jnp.where(which == line, value.astype(jnp.float32), column)
    return jnp.concatenate(columns, axis=1).astype(jnp.bfloat16)


def start_kernel(
    odd_ref, hidden_in_ref, regular_in_ref, shifted_in_ref, w_in_ref, near_ref, far_ref, query_ref,
    key_ref, value_ref, hidden_ref, w_qkv_ref, parity_ref, regular_ref, shifted_ref, sems,
):
    rows, channels = hidden_ref.shape
    rim = rows // 4
    copies = [
        pltpu.make_async_copy(hidden_in_ref, hidden_ref, sems.at[0]),
        pltpu.make_async_copy(w_in_ref.at[pl.ds(0, 1)], w_qkv_ref, sems.at[1]),
        pltpu.make_async_copy(regular_in_ref, regular_ref, sems.at[2]),
        pltpu.make_async_copy(shifted_in_ref, shifted_ref, sems.at[3]),
    ]
    for copy in copies:
        copy.start()
    for copy in copies:
        copy.wait()
    odd = odd_ref[0]
    parity_ref[...] = jnp.full(parity_ref.shape, odd, jnp.int32)
    for out_ref, at_end in ((near_ref, 1 - odd), (far_ref, odd)):
        start = pl.multiple_of(at_end * (rows - rim), TILE)
        out_ref[:rim] = hidden_ref[pl.ds(start, rim)]
        out_ref[rim:] = tail_of(
            (regular_ref, shifted_ref), at_end * ((rows - rim) // TILE), rim, channels
        )
    project(0, hidden_ref, w_qkv_ref, query_ref, key_ref, value_ref)


def run_start(odd, hidden, regular, shifted, w_qkv):
    rows, channels = hidden.shape
    edge = pltpu.VMEM((rows // 4 + TAIL, channels), jnp.bfloat16)
    return pl.pallas_call(
        start_kernel,
        out_shape=(
            edge,
            edge,
            *[pltpu.VMEM(x.shape, x.dtype) for x in projected_shapes(rows, channels)],
            pltpu.VMEM(hidden.shape, hidden.dtype),
            pltpu.VMEM((1,) + w_qkv.shape[1:], w_qkv.dtype),
            pltpu.VMEM((8, TILE), jnp.int32),
        ),
        in_specs=[smem] + [hbm] * 4,
        out_specs=(vmem,) * 8,
        scratch_shapes=[
            pltpu.VMEM((rows // TILE, TILE), jnp.int32),
            pltpu.VMEM((rows // TILE, TILE), jnp.int32),
            pltpu.SemaphoreType.DMA((4,)),
        ],

        name="start",
    )(odd, hidden, regular.reshape(-1, TILE), shifted.reshape(-1, TILE), w_qkv)


def attend_kernel(
    layer, far, packing, odd_ref, temper_ref, marks_own_ref, tail_ref, halo_ref,
    hidden_ref, query_ref, key_own_ref, value_own_ref, w_qkv_ref, w_out_ref, gain_ref, *refs,
):
    if far:
        done_ref, dest_ref, *refs = refs
    (
        out_ref, span_ref, marks_ref, column_ref, key_ref, value_ref, bound_ref, attended_ref,
        first_ref, least_ref, *sems,
    ) = refs
    rows, channels = hidden_ref.shape
    rim = rows // 4
    rim_tiles, own_tiles = rim // TILE, rows // TILE
    in_view = 2 * rim if far else rows
    odd = jnp.max(odd_ref[...])
    at_end = odd if far else 1 - odd
    own_tile = at_end * ((rows - in_view) // TILE)
    own_at = (1 - at_end) * rim_tiles
    halo_at = at_end * (in_view // TILE)
    count = rim_tiles if far else own_tiles - rim_tiles
    first_tile = at_end * (own_tiles - count)
    factor = (1.0 / math.sqrt(channels // HEADS)) * math.log2(math.e)
    scales = [temper_ref[layer : layer + 1, j : j + 1] * factor for j in range(HEADS)]

    if sems:
        other = pl.ds(pl.multiple_of((1 - at_end) * rim, TILE), rows - rim)
        rest = pltpu.make_async_copy(done_ref.at[other], out_ref.at[other], sems[0].at[0])
        rest.start()

    past_end = jnp.max(marks_own_ref[...]) + 2
    halo = halo_marks(tail_ref[rim : rim + TAIL].astype(jnp.float32), layer, rim)
    halo = [jnp.where((m == 0) & (at_end == 1), past_end, m) for m in halo]
    marks_ref[pl.ds(own_at, in_view // TILE), :] = (
        marks_own_ref[pl.ds(own_tile, in_view // TILE), :] + 1
    )
    for i in range(rim_tiles):
        marks_ref[pl.ds(halo_at + i, 1), :] = halo[i]
    begins, ends = [], []
    for i in range(marks_ref.shape[0]):
        marks = marks_ref[i : i + 1]
        begins.append(jnp.min(marks))
        ends.append(jnp.max(marks))
    for number in range(count):
        marks = marks_own_ref[pl.ds(first_tile + number, 1), :] + 1
        lowest, highest = jnp.min(marks), jnp.max(marks)
        begin, end = jnp.int32(0), jnp.int32(0)
        for i in range(len(begins)):
            begin += (ends[i] < lowest).astype(jnp.int32)
            end += (begins[i] <= highest).astype(jnp.int32)
        span_ref[0, number] = begin
        span_ref[1, number] = end - begin
    for i in range(marks_ref.shape[0]):
        column_ref[i * TILE : (i + 1) * TILE] = jnp.transpose(
            jnp.broadcast_to(marks_ref[i : i + 1, :], (TILE, TILE))
        )

    there = pl.ds(pl.multiple_of(own_at * TILE, TILE), in_view)
    own = pl.ds(pl.multiple_of(own_tile * TILE, TILE), in_view)
    key_ref[there] = key_own_ref[own]
    value_ref[:, there] = value_own_ref[:, own]
    there = pl.ds(pl.multiple_of(halo_at * TILE, TILE), rim)
    source = halo_ref[:rim]
    w_value = jnp.transpose(w_qkv_ref[w_qkv_ref.shape[0] - 1, :, 2 * channels :])
    key_ref[there] = dot(source, w_qkv_ref[w_qkv_ref.shape[0] - 1, :, channels : 2 * channels]).astype(jnp.bfloat16)
    value_ref[:, there] = dot_t(w_value, source).astype(jnp.bfloat16)
    wanted = pl.ds(pl.multiple_of(first_tile * TILE, TILE), count * TILE)
    bound_scores(scales, query_ref, key_ref, bound_ref, wanted)
    shared = (span_ref, scales, marks_own_ref, column_ref, bound_ref, query_ref, key_ref, value_ref)

    def one_tile(number, nothing):
        attend_tile(number, first_tile, *shared, attended_ref, least_ref, rim)
        return nothing

    lax.fori_loop(0, count, one_tile, 0)

    loose = jnp.logical_not(jnp.min(least_ref[...]) >= fewest)
    final_ref = first_ref if far else out_ref
    if far and packing:
        other_tile = (1 - at_end) * rim_tiles
        other = pl.ds(pl.multiple_of(other_tile * TILE, TILE), rows - rim)
        final_ref[other] = done_ref[other]
    def finish():
        for number in range(count):
            here = pl.ds(pl.multiple_of((first_tile + number) * TILE, TILE), TILE)
            attended = jnp.transpose(attended_ref[number]).astype(jnp.bfloat16)
            summed = hidden_ref[here].astype(jnp.float32) + dot(attended, w_out_ref[layer])
            center = jnp.mean(summed, axis=1, keepdims=True)
            summed = summed - center
            spread = jnp.mean(jnp.square(summed), axis=1, keepdims=True)
            scaled = summed * lax.rsqrt(spread + epsilon) * gain_ref[layer : layer + 1]
            final_ref[here] = scaled.astype(jnp.bfloat16)

    finish()

    @pl.when(loose)
    def some_again():
        def one_again(number, nothing):
            @pl.when(jnp.logical_not(jnp.min(least_ref[pl.ds(number, 1), :]) >= fewest))
            def again():
                attend_tile(number, first_tile, *shared, attended_ref, None, rim)

            return nothing

        lax.fori_loop(0, count, one_again, 0)
        finish()

    if packing:
        pack(packing, dest_ref, first_ref, out_ref)
    if sems:
        mine = pl.ds(pl.multiple_of(first_tile * TILE, TILE), rim)
        last = pltpu.make_async_copy(first_ref.at[mine], out_ref.at[mine], sems[0].at[1])
        last.start()
        rest.wait()
        last.wait()


def pack(devices, dest_ref, first_ref, out_ref):
    rows, channels = first_ref.shape
    capacity = 2 * rows // devices
    dest = jnp.concatenate([dest_ref[i : i + 1] for i in range(rows // TILE)], axis=1)
    target = dest // rows
    match = jnp.where(lax.broadcasted_iota(jnp.int32, (devices, rows), 0) == target, 1.0, 0.0)
    rank = jnp.sum(ranks(match) * match, axis=0, keepdims=True).astype(jnp.int32)
    slot = (dest - target * rows).astype(jnp.int32)
    digits = [match * (slot // 32 + 1).astype(jnp.float32), match * (slot % 32).astype(jnp.float32)]
    digits = jnp.concatenate(digits, axis=0).astype(jnp.bfloat16)
    at_rank = one_hot(lax.broadcasted_iota(jnp.int32, (capacity, rows), 0) == rank)
    slots = dot_t(digits, at_rank)
    if capacity < TILE:
        blank = jnp.zeros((2 * devices, TILE - capacity), jnp.float32)
        slots = jnp.concatenate([slots, blank], axis=1)
    slots = jnp.concatenate([slots[:devices], slots[devices:]], axis=1)
    for i in range(devices):
        line = jnp.broadcast_to(slots[i : i + 1], (8, channels)).astype(jnp.bfloat16)
        out_ref[i, capacity:] = line
    place = rank + target * capacity
    together = max(1, 512 // capacity)
    index = lax.broadcasted_iota(jnp.int32, (together * capacity, rows), 0)
    for start in range(0, devices, together):
        hits = one_hot(index == place - start * capacity)
        packed = dot(hits, first_ref[...]).astype(jnp.bfloat16)
        for i in range(together):
            out_ref[start + i, :capacity] = packed[i * capacity : (i + 1) * capacity]


def run_attend(layer, far, packing, operands, more=()):
    rows, channels = operands[5].shape
    rim = rows // 4
    tiles = rows // TILE
    count = rim // TILE if far else tiles - rim // TILE
    view = rim + (2 * rim if far else rows)
    shape = (packing, 2 * rows // packing + 8, channels) if packing else (rows, channels)
    return pl.pallas_call(
        functools.partial(attend_kernel, layer, far, packing),
        out_shape=jax.ShapeDtypeStruct(shape, jnp.bfloat16),
        in_specs=[vmem] * (len(operands) + len(more)),
        out_specs=hbm if far and not packing else vmem,
        scratch_shapes=[
            pltpu.SMEM((2, count), jnp.int32),
            pltpu.VMEM((view // TILE, TILE), jnp.int32),
            pltpu.VMEM((view, TILE), jnp.int32),
            pltpu.VMEM((view, channels), jnp.bfloat16),
            pltpu.VMEM((channels, view), jnp.bfloat16),
            pltpu.VMEM((HEADS, rows), jnp.float32),
            pltpu.VMEM((count, channels, TILE), jnp.float32),
            pltpu.VMEM((rows, channels), jnp.bfloat16),
            pltpu.VMEM((count, TILE), jnp.float32),
        ]
        + ([pltpu.SemaphoreType.DMA((2,))] if far and not packing else []),
        compiler_params=pltpu.CompilerParams(vmem_limit_bytes=vmem_limit),
        cost_estimate=pl.CostEstimate(
            flops=10**9 * count, bytes_accessed=4 * 10**6, transcendentals=10**6 * count
        ),
        name="far" if far else "near",
    )(*operands, *more)


def run_sublayer(layer, packing, odd, temper, window, dest, tails, near, far, hidden, projected, weights):
    marks = window.reshape(-1, TILE)

    def operands(tail, halo):
        return (odd, temper, marks, tail, halo, hidden, *projected, *weights)

    done = run_attend(layer, False, 0, operands(tails[0], near))
    return run_attend(
        layer, True, packing, operands(tails[1], far), (done, dest.reshape(-1, TILE))
    )


def place_kernel(odd_ref, arrived_ref, w_qkv_ref, moved_ref, near_ref, far_ref, *projected_refs):
    odd = jnp.max(odd_ref[...])
    rows = moved_ref.shape[0]
    rim = near_ref.shape[0]
    devices, padded, channels = arrived_ref.shape
    capacity = padded - 8
    slots = []
    for i in range(devices):
        line = arrived_ref[i, capacity:].astype(jnp.float32)
        value = line[0:1, :capacity] * 32.0 + line[0:1, TILE : TILE + capacity] - 32.0
        slots.append(value.astype(jnp.int32))
    arrived = jnp.concatenate([arrived_ref[i, :capacity] for i in range(devices)], axis=0)
    chunk = min(256, rows)
    for start in range(0, rows, chunk):
        index = lax.broadcasted_iota(jnp.int32, (chunk, capacity), 0) + start
        hits = jnp.concatenate([one_hot(index == slots[i]) for i in range(devices)], axis=1)
        moved_ref[start : start + chunk] = dot(hits, arrived).astype(jnp.bfloat16)
    project(1, moved_ref, w_qkv_ref, *projected_refs)
    for out_ref, at_end in ((near_ref, 1 - odd), (far_ref, odd)):
        out_ref[...] = moved_ref[pl.ds(pl.multiple_of(at_end * (rows - rim), TILE), rim)]


def run_place(odd, arrived, rows, w_qkv):
    channels = arrived.shape[2]
    edge = jax.ShapeDtypeStruct((rows // 4, channels), jnp.bfloat16)
    moved = jax.ShapeDtypeStruct((rows, channels), jnp.bfloat16)
    return pl.pallas_call(
        place_kernel,
        out_shape=(moved, edge, edge, *projected_shapes(rows, channels)),
        in_specs=[vmem] * 3,
        out_specs=(vmem,) * 6,
        compiler_params=pltpu.CompilerParams(vmem_limit_bytes=vmem_limit),
        cost_estimate=pl.CostEstimate(
            flops=10**9, bytes_accessed=2 * 10**6, transcendentals=0
        ),
        name="place",
    )(odd, arrived, w_qkv)


def exchange(near, far):
    count = lax.axis_size("wide")
    inner = [(i, i + 1) for i in range(0, count - 1, 2)]
    outer = [(i, i + 1) for i in range(1, count - 1, 2)]
    far = lax.ppermute(far, "wide", outer + [(b, a) for a, b in outer])
    near = lax.ppermute(near, "wide", inner + [(b, a) for a, b in inner])
    return near, far


def body(voxels, regular_window, shifted_window, dest, w_qkv, w_out, gain, temper):
    rows, channels = voxels.shape
    devices = lax.axis_size("wide")
    odd = lax.axis_index("wide").astype(jnp.int32) % 2
    near, far, *projected, hidden, w_first, odd = run_start(
        odd.reshape(1), voxels, regular_window, shifted_window, w_qkv
    )
    tails = exchange(near, far)
    outgoing = run_sublayer(
        0, devices, odd, temper, regular_window, dest, tails, *tails, hidden, projected,
        (w_first, w_out, gain),
    )
    arrived = lax.all_to_all(outgoing, "wide", split_axis=0, concat_axis=0, tiled=True)
    moved, near, far, *projected = run_place(odd, arrived, rows, w_qkv)
    near, far = exchange(near, far)
    return run_sublayer(
        1, 0, odd, temper, shifted_window, dest, tails, near, far, moved, projected,
        (w_qkv, w_out, gain),
    )


def solution(mesh):
    in_specs = (
        P(("parts", "wide"), None),
        P(("parts", "wide")),
        P(("parts", "wide")),
        P(("parts", "wide")),
        P(),
        P(),
        P(),
        P(),
    )
    out_specs = P(("parts", "wide"), None)
    return jax.shard_map(body, mesh=mesh, in_specs=in_specs, out_specs=out_specs, check_vma=False)
```

```python
import functools
import math

import jax
import jax.numpy as jnp
from jax import lax
from jax.experimental import pallas as pl
from jax.experimental.pallas import tpu as pltpu
from jax.sharding import PartitionSpec as P

HEADS = 8
TILE = 128
TAIL = 16

epsilon = 1e-05
masked_score = -1e30
fewest = 2.0**-100
no_mark = 1 << 30
vmem_limit = 40 * 1024 * 1024

vmem = pl.BlockSpec(memory_space=pltpu.VMEM)
hbm = pl.BlockSpec(memory_space=pltpu.HBM)
smem = pl.BlockSpec(memory_space=pltpu.SMEM)


def dot(a, b):
    return jnp.dot(a, b, preferred_element_type=jnp.float32)


def dot_t(a, b):
    return lax.dot_general(a, b, (((1,), (1,)), ((), ())), preferred_element_type=jnp.float32)


def one_hot(hits):
    return jnp.where(hits, 1.0, 0.0).astype(jnp.bfloat16)


def ranks(match):
    rows, columns = match.shape
    before = one_hot(
        lax.broadcasted_iota(jnp.int32, (TILE, TILE), 0)
        < lax.broadcasted_iota(jnp.int32, (TILE, TILE), 1)
    )
    carry = jnp.zeros((rows, 1), jnp.float32)
    pieces = []
    for start in range(0, columns, TILE):
        piece = match[:, start : start + TILE]
        pieces.append(dot(piece.astype(jnp.bfloat16), before) + carry)
        carry = carry + jnp.sum(piece, axis=1, keepdims=True)
    return jnp.concatenate(pieces, axis=1)


def project(layer, hidden_ref, w_qkv_ref, query_ref, key_ref, value_ref):
    rows, channels = hidden_ref.shape
    chunk = min(256, rows)
    w_query = jnp.transpose(w_qkv_ref[layer, :, :channels])
    w_value = jnp.transpose(w_qkv_ref[layer, :, 2 * channels :])
    w_both = jnp.concatenate([w_query, w_value], axis=0)
    for start in range(0, rows, chunk):
        here = slice(start, start + chunk)
        source = hidden_ref[here]
        key_ref[here] = dot(source, w_qkv_ref[layer, :, channels : 2 * channels]).astype(
            jnp.bfloat16
        )
        both = dot_t(w_both, source).astype(jnp.bfloat16)
        query_ref[:, here] = both[:channels]
        value_ref[:, here] = both[channels:]


def projected_shapes(rows, channels):
    return (
        jax.ShapeDtypeStruct((channels, rows), jnp.bfloat16),
        jax.ShapeDtypeStruct((rows, channels), jnp.bfloat16),
        jax.ShapeDtypeStruct((channels, rows), jnp.bfloat16),
    )


def bound_scores(scales, query_ref, key_ref, bound_ref, wanted):
    channels = query_ref.shape[0]
    head_dim = channels // HEADS
    column = lax.broadcasted_iota(jnp.int32, (channels, TILE), 0)
    first = lax.broadcasted_iota(jnp.int32, (channels, TILE), 1) * head_dim
    heads = one_hot((column >= first) & (column < first + head_dim))
    norm = jnp.zeros((1, TILE), jnp.float32)
    for start in range(0, key_ref.shape[0], 2 * TILE):
        keys = key_ref[start : start + 2 * TILE].astype(jnp.float32)
        lengths = dot((keys * keys).astype(jnp.bfloat16), heads)
        norm = jnp.maximum(norm, jnp.max(lengths, axis=0, keepdims=True))
    lane = lax.broadcasted_iota(jnp.int32, (1, TILE), 1)
    for j in range(HEADS):
        query = query_ref[j * head_dim : (j + 1) * head_dim, wanted].astype(jnp.float32)
        length = jnp.sum(query * query, axis=0, keepdims=True)
        longest = jnp.sum(jnp.where(lane == j, norm, 0.0), axis=1, keepdims=True)
        bound_ref[j : j + 1, wanted] = jnp.sqrt(length * longest) * (scales[j] * -1.01)


def attend_tile(
    number, first_tile, span_ref, scales, marks_own_ref, column_ref, bound_ref, query_ref, key_ref,
    value_ref, attended_ref, least_ref, rim,
):
    channels = query_ref.shape[0]
    head_dim = channels // HEADS
    per_group = TILE // head_dim
    tile = first_tile + number
    here = pl.ds(pl.multiple_of(tile * TILE, TILE), TILE)
    most = 1 + 2 * (rim // TILE)
    blank = jnp.zeros((head_dim, TILE), jnp.bfloat16)
    exact = least_ref is None

    def variant(low, tiles):
        span = pl.ds(pl.multiple_of(low * TILE, TILE), tiles * TILE)
        own = marks_own_ref[pl.ds(tile, 1), :] + 1
        bias = jnp.where(column_ref[span, :] == own, 0.0, masked_score)
        parts = []
        for j in range(HEADS):
            group = j // per_group
            column = [blank] * per_group
            column[j % per_group] = query_ref[j * head_dim : (j + 1) * head_dim, here]
            keys = key_ref[span, group * TILE : (group + 1) * TILE]
            parts.append(dot(keys, jnp.concatenate(column, axis=0)))
        least = None
        for j in range(HEADS):
            if exact:
                part = parts[j] * scales[j] + bias
                part = jnp.exp2(part - jnp.max(part, axis=0, keepdims=True))
            else:
                part = jnp.exp2(parts[j] * scales[j] + (bias + bound_ref[j : j + 1, here]))
            total = jnp.sum(part, axis=0, keepdims=True)
            least = total if j == 0 else jnp.minimum(least, total)
            parts[j] = (part * (1.0 / total)).astype(jnp.bfloat16)
        for j in range(HEADS):
            begin = j * head_dim
            mixed = dot(value_ref[begin : begin + head_dim, span], parts[j])
            attended_ref[pl.ds(number, 1), begin : begin + head_dim] = mixed[None]
        if not exact:
            least_ref[pl.ds(number, 1), :] = least

    low = span_ref[0, number]
    if exact:
        variant(jnp.minimum(low, key_ref.shape[0] // TILE - most), most)
        return
    for tiles in range(2, most + 1):
        pl.when(jnp.maximum(span_ref[1, number], 2) == tiles)(
            functools.partial(variant, low, tiles)
        )


def mark_place(layer, digit, start, rim, channels):
    place = (2 * layer + digit) * rim + start
    return place // channels, place % channels


def halo_marks(tail, layer, rim):
    found = []
    for start in range(0, rim, TILE):
        digits = []
        for digit in range(2):
            line, lane = mark_place(layer, digit, start, rim, tail.shape[1])
            digits.append(tail[line : line + 1, lane : lane + TILE])
        found.append((digits[0] * 256.0 + digits[1]).astype(jnp.int32))
    return found


def tail_of(windows_refs, first_tile, rim, channels):
    which = lax.broadcasted_iota(jnp.int32, (TAIL, TILE), 0)
    columns = [jnp.zeros((TAIL, TILE), jnp.float32) for _ in range(channels // TILE)]
    for layer, window_ref in enumerate(windows_refs):
        for start in range(0, rim, TILE):
            mark = window_ref[pl.ds(first_tile + start // TILE, 1), :] + 1
            for digit, value in enumerate((mark // 256, mark % 256)):
                line, lane = mark_place(layer, digit, start, rim, channels)
                column = columns[lane // TILE]
                columns[lane // TILE] = jnp.where(which == line, value.astype(jnp.float32), column)
    return jnp.concatenate(columns, axis=1).astype(jnp.bfloat16)


def start_kernel(
    devices, odd_ref, hidden_in_ref, regular_in_ref, shifted_in_ref, dest_in_ref, w_in_ref, near_ref, far_ref, query_ref,
    key_ref, value_ref, hidden_ref, w_qkv_ref, parity_ref, place_ref, line_ref, regular_ref, shifted_ref, dest_ref, sems,
):
    rows, channels = hidden_ref.shape
    rim = rows // 4
    copies = [
        pltpu.make_async_copy(hidden_in_ref, hidden_ref, sems.at[0]),
        pltpu.make_async_copy(w_in_ref.at[pl.ds(0, 1)], w_qkv_ref, sems.at[1]),
        pltpu.make_async_copy(regular_in_ref, regular_ref, sems.at[2]),
        pltpu.make_async_copy(shifted_in_ref, shifted_ref, sems.at[3]),
        pltpu.make_async_copy(dest_in_ref, dest_ref, sems.at[4]),
    ]
    for copy in copies[2:] + copies[:2]:
        copy.start()
    for copy in copies[2:]:
        copy.wait()
    find_places(devices, channels, dest_ref, place_ref, line_ref)
    odd = odd_ref[0]
    parity_ref[...] = jnp.full(parity_ref.shape, odd, jnp.int32)
    ends = ((near_ref, 1 - odd), (far_ref, odd))
    for out_ref, at_end in ends:
        out_ref[rim:] = tail_of(
            (regular_ref, shifted_ref), at_end * ((rows - rim) // TILE), rim, channels
        )
    for copy in copies[:2]:
        copy.wait()
    for out_ref, at_end in ends:
        out_ref[:rim] = hidden_ref[pl.ds(pl.multiple_of(at_end * (rows - rim), TILE), rim)]
    project(0, hidden_ref, w_qkv_ref, query_ref, key_ref, value_ref)


def run_start(devices, odd, hidden, regular, shifted, dest, w_qkv):
    rows, channels = hidden.shape
    edge = pltpu.VMEM((rows // 4 + TAIL, channels), jnp.bfloat16)
    return pl.pallas_call(
        functools.partial(start_kernel, devices),
        out_shape=(
            edge,
            edge,
            *[pltpu.VMEM(x.shape, x.dtype) for x in projected_shapes(rows, channels)],
            pltpu.VMEM(hidden.shape, hidden.dtype),
            pltpu.VMEM((1,) + w_qkv.shape[1:], w_qkv.dtype),
            pltpu.VMEM((8, TILE), jnp.int32),
            pltpu.VMEM((1, rows), jnp.int32),
            pltpu.VMEM((devices, 8, channels), jnp.bfloat16),
        ),
        in_specs=[smem] + [hbm] * 5,
        out_specs=(vmem,) * 10,
        scratch_shapes=[
            pltpu.VMEM((rows // TILE, TILE), jnp.int32),
            pltpu.VMEM((rows // TILE, TILE), jnp.int32),
            pltpu.VMEM((rows // TILE, TILE), jnp.int32),
            pltpu.SemaphoreType.DMA((5,)),
        ],

        name="start",
    )(
        odd, hidden, regular.reshape(-1, TILE), shifted.reshape(-1, TILE), dest.reshape(-1, TILE),
        w_qkv,
    )


def attend_kernel(
    layer, far, packing, odd_ref, temper_ref, marks_own_ref, tail_ref, halo_ref,
    hidden_ref, query_ref, key_own_ref, value_own_ref, w_qkv_ref, w_out_ref, gain_ref, *refs,
):
    if far:
        done_ref, place_ref, line_ref, *refs = refs
    (
        out_ref, span_ref, marks_ref, column_ref, key_ref, value_ref, bound_ref, attended_ref,
        first_ref, least_ref, *sems,
    ) = refs
    rows, channels = hidden_ref.shape
    rim = rows // 4
    rim_tiles, own_tiles = rim // TILE, rows // TILE
    in_view = 2 * rim if far else rows
    odd = jnp.max(odd_ref[...])
    at_end = odd if far else 1 - odd
    own_tile = at_end * ((rows - in_view) // TILE)
    own_at = (1 - at_end) * rim_tiles
    halo_at = at_end * (in_view // TILE)
    count = rim_tiles if far else own_tiles - rim_tiles
    first_tile = at_end * (own_tiles - count)
    factor = (1.0 / math.sqrt(channels // HEADS)) * math.log2(math.e)
    scales = [temper_ref[layer : layer + 1, j : j + 1] * factor for j in range(HEADS)]

    if sems:
        other = pl.ds(pl.multiple_of((1 - at_end) * rim, TILE), rows - rim)
        rest = pltpu.make_async_copy(done_ref.at[other], out_ref.at[other], sems[0].at[0])
        rest.start()

    past_end = jnp.max(marks_own_ref[...]) + 2
    halo = halo_marks(tail_ref[rim : rim + TAIL].astype(jnp.float32), layer, rim)
    halo = [jnp.where((m == 0) & (at_end == 1), past_end, m) for m in halo]
    marks_ref[pl.ds(own_at, in_view // TILE), :] = (
        marks_own_ref[pl.ds(own_tile, in_view // TILE), :] + 1
    )
    for i in range(rim_tiles):
        marks_ref[pl.ds(halo_at + i, 1), :] = halo[i]
    begins, ends = [], []
    for i in range(marks_ref.shape[0]):
        marks = marks_ref[i : i + 1]
        begins.append(jnp.min(marks))
        ends.append(jnp.max(marks))
    for number in range(count):
        marks = marks_own_ref[pl.ds(first_tile + number, 1), :] + 1
        lowest, highest = jnp.min(marks), jnp.max(marks)
        begin, end = jnp.int32(0), jnp.int32(0)
        for i in range(len(begins)):
            begin += (ends[i] < lowest).astype(jnp.int32)
            end += (begins[i] <= highest).astype(jnp.int32)
        span_ref[0, number] = begin
        span_ref[1, number] = end - begin
    for i in range(marks_ref.shape[0]):
        column_ref[i * TILE : (i + 1) * TILE] = jnp.transpose(
            jnp.broadcast_to(marks_ref[i : i + 1, :], (TILE, TILE))
        )

    there = pl.ds(pl.multiple_of(own_at * TILE, TILE), in_view)
    own = pl.ds(pl.multiple_of(own_tile * TILE, TILE), in_view)
    key_ref[there] = key_own_ref[own]
    value_ref[:, there] = value_own_ref[:, own]
    there = pl.ds(pl.multiple_of(halo_at * TILE, TILE), rim)
    source = halo_ref[:rim]
    w_value = jnp.transpose(w_qkv_ref[w_qkv_ref.shape[0] - 1, :, 2 * channels :])
    key_ref[there] = dot(source, w_qkv_ref[w_qkv_ref.shape[0] - 1, :, channels : 2 * channels]).astype(jnp.bfloat16)
    value_ref[:, there] = dot_t(w_value, source).astype(jnp.bfloat16)
    wanted = pl.ds(pl.multiple_of(first_tile * TILE, TILE), count * TILE)
    bound_scores(scales, query_ref, key_ref, bound_ref, wanted)
    shared = (span_ref, scales, marks_own_ref, column_ref, bound_ref, query_ref, key_ref, value_ref)

    def one_tile(number, nothing):
        attend_tile(number, first_tile, *shared, attended_ref, least_ref, rim)
        return nothing

    lax.fori_loop(0, count, one_tile, 0)

    loose = jnp.logical_not(jnp.min(least_ref[...]) >= fewest)
    final_ref = first_ref if far else out_ref
    if far and packing:
        other_tile = (1 - at_end) * rim_tiles
        other = pl.ds(pl.multiple_of(other_tile * TILE, TILE), rows - rim)
        final_ref[other] = done_ref[other]
    def finish():
        for number in range(count):
            here = pl.ds(pl.multiple_of((first_tile + number) * TILE, TILE), TILE)
            attended = jnp.transpose(attended_ref[number]).astype(jnp.bfloat16)
            summed = hidden_ref[here].astype(jnp.float32) + dot(attended, w_out_ref[layer])
            center = jnp.mean(summed, axis=1, keepdims=True)
            summed = summed - center
            spread = jnp.mean(jnp.square(summed), axis=1, keepdims=True)
            scaled = summed * lax.rsqrt(spread + epsilon) * gain_ref[layer : layer + 1]
            final_ref[here] = scaled.astype(jnp.bfloat16)

    finish()

    @pl.when(loose)
    def some_again():
        def one_again(number, nothing):
            @pl.when(jnp.logical_not(jnp.min(least_ref[pl.ds(number, 1), :]) >= fewest))
            def again():
                attend_tile(number, first_tile, *shared, attended_ref, None, rim)

            return nothing

        lax.fori_loop(0, count, one_again, 0)
        finish()

    if packing:
        pack(packing, place_ref, line_ref, first_ref, out_ref)
    if sems:
        mine = pl.ds(pl.multiple_of(first_tile * TILE, TILE), rim)
        last = pltpu.make_async_copy(first_ref.at[mine], out_ref.at[mine], sems[0].at[1])
        last.start()
        rest.wait()
        last.wait()


def find_places(devices, channels, dest_ref, place_ref, line_ref):
    rows = dest_ref.shape[0] * TILE
    capacity = 2 * rows // devices
    dest = jnp.concatenate([dest_ref[i : i + 1] for i in range(rows // TILE)], axis=1)
    target = dest // rows
    match = jnp.where(lax.broadcasted_iota(jnp.int32, (devices, rows), 0) == target, 1.0, 0.0)
    rank = jnp.sum(ranks(match) * match, axis=0, keepdims=True).astype(jnp.int32)
    slot = (dest - target * rows).astype(jnp.int32)
    digits = [match * (slot // 32 + 1).astype(jnp.float32), match * (slot % 32).astype(jnp.float32)]
    digits = jnp.concatenate(digits, axis=0).astype(jnp.bfloat16)
    at_rank = one_hot(lax.broadcasted_iota(jnp.int32, (capacity, rows), 0) == rank)
    slots = dot_t(digits, at_rank)
    if capacity < TILE:
        blank = jnp.zeros((2 * devices, TILE - capacity), jnp.float32)
        slots = jnp.concatenate([slots, blank], axis=1)
    slots = jnp.concatenate([slots[:devices], slots[devices:]], axis=1)
    for i in range(devices):
        line = jnp.broadcast_to(slots[i : i + 1], (8, channels)).astype(jnp.bfloat16)
        line_ref[i] = line
    place_ref[...] = rank + target * capacity


def pack(devices, place_ref, line_ref, first_ref, out_ref):
    rows = first_ref.shape[0]
    capacity = 2 * rows // devices
    place = place_ref[...]
    for i in range(devices):
        out_ref[i, capacity:] = line_ref[i]
    together = max(1, 512 // capacity)
    index = lax.broadcasted_iota(jnp.int32, (together * capacity, rows), 0)
    for start in range(0, devices, together):
        hits = one_hot(index == place - start * capacity)
        packed = dot(hits, first_ref[...]).astype(jnp.bfloat16)
        for i in range(together):
            out_ref[start + i, :capacity] = packed[i * capacity : (i + 1) * capacity]


def run_attend(layer, far, packing, operands, more=()):
    rows, channels = operands[5].shape
    rim = rows // 4
    tiles = rows // TILE
    count = rim // TILE if far else tiles - rim // TILE
    view = rim + (2 * rim if far else rows)
    shape = (packing, 2 * rows // packing + 8, channels) if packing else (rows, channels)
    return pl.pallas_call(
        functools.partial(attend_kernel, layer, far, packing),
        out_shape=jax.ShapeDtypeStruct(shape, jnp.bfloat16),
        in_specs=[vmem] * (len(operands) + len(more)),
        out_specs=hbm if far and not packing else vmem,
        scratch_shapes=[
            pltpu.SMEM((2, count), jnp.int32),
            pltpu.VMEM((view // TILE, TILE), jnp.int32),
            pltpu.VMEM((view, TILE), jnp.int32),
            pltpu.VMEM((view, channels), jnp.bfloat16),
            pltpu.VMEM((channels, view), jnp.bfloat16),
            pltpu.VMEM((HEADS, rows), jnp.float32),
            pltpu.VMEM((count, channels, TILE), jnp.float32),
            pltpu.VMEM((rows, channels), jnp.bfloat16),
            pltpu.VMEM((count, TILE), jnp.float32),
        ]
        + ([pltpu.SemaphoreType.DMA((2,))] if far and not packing else []),
        compiler_params=pltpu.CompilerParams(vmem_limit_bytes=vmem_limit),
        cost_estimate=pl.CostEstimate(
            flops=10**9 * count, bytes_accessed=4 * 10**6, transcendentals=10**6 * count
        ),
        name="far" if far else "near",
    )(*operands, *more)


def run_sublayer(layer, packing, odd, temper, window, places, tails, near, far, hidden, projected, weights):
    marks = window.reshape(-1, TILE)

    def operands(tail, halo):
        return (odd, temper, marks, tail, halo, hidden, *projected, *weights)

    done = run_attend(layer, False, 0, operands(tails[0], near))
    return run_attend(
        layer, True, packing, operands(tails[1], far), (done, *places)
    )


def place_kernel(odd_ref, arrived_ref, w_qkv_ref, moved_ref, near_ref, far_ref, *projected_refs):
    odd = jnp.max(odd_ref[...])
    rows = moved_ref.shape[0]
    rim = near_ref.shape[0]
    devices, padded, channels = arrived_ref.shape
    capacity = padded - 8
    slots = []
    for i in range(devices):
        line = arrived_ref[i, capacity:].astype(jnp.float32)
        value = line[0:1, :capacity] * 32.0 + line[0:1, TILE : TILE + capacity] - 32.0
        slots.append(value.astype(jnp.int32))
    arrived = jnp.concatenate([arrived_ref[i, :capacity] for i in range(devices)], axis=0)
    chunk = min(256, rows)
    for start in range(0, rows, chunk):
        index = lax.broadcasted_iota(jnp.int32, (chunk, capacity), 0) + start
        hits = jnp.concatenate([one_hot(index == slots[i]) for i in range(devices)], axis=1)
        moved_ref[start : start + chunk] = dot(hits, arrived).astype(jnp.bfloat16)
    project(1, moved_ref, w_qkv_ref, *projected_refs)
    for out_ref, at_end in ((near_ref, 1 - odd), (far_ref, odd)):
        out_ref[...] = moved_ref[pl.ds(pl.multiple_of(at_end * (rows - rim), TILE), rim)]


def run_place(odd, arrived, rows, w_qkv):
    channels = arrived.shape[2]
    edge = jax.ShapeDtypeStruct((rows // 4, channels), jnp.bfloat16)
    moved = jax.ShapeDtypeStruct((rows, channels), jnp.bfloat16)
    return pl.pallas_call(
        place_kernel,
        out_shape=(moved, edge, edge, *projected_shapes(rows, channels)),
        in_specs=[vmem] * 3,
        out_specs=(vmem,) * 6,
        compiler_params=pltpu.CompilerParams(vmem_limit_bytes=vmem_limit),
        cost_estimate=pl.CostEstimate(
            flops=10**9, bytes_accessed=2 * 10**6, transcendentals=0
        ),
        name="place",
    )(odd, arrived, w_qkv)


def exchange(near, far):
    count = lax.axis_size("wide")
    inner = [(i, i + 1) for i in range(0, count - 1, 2)]
    outer = [(i, i + 1) for i in range(1, count - 1, 2)]
    far = lax.ppermute(far, "wide", outer + [(b, a) for a, b in outer])
    near = lax.ppermute(near, "wide", inner + [(b, a) for a, b in inner])
    return near, far


def body(voxels, regular_window, shifted_window, dest, w_qkv, w_out, gain, temper):
    rows, channels = voxels.shape
    devices = lax.axis_size("wide")
    odd = lax.axis_index("wide").astype(jnp.int32) % 2
    near, far, *projected, hidden, w_first, odd, place, line = run_start(
        devices, odd.reshape(1), voxels, regular_window, shifted_window, dest, w_qkv
    )
    places = (place, line)
    tails = exchange(near, far)
    outgoing = run_sublayer(
        0, devices, odd, temper, regular_window, places, tails, *tails, hidden, projected,
        (w_first, w_out, gain),
    )
    arrived = lax.all_to_all(outgoing, "wide", split_axis=0, concat_axis=0, tiled=True)
    moved, near, far, *projected = run_place(odd, arrived, rows, w_qkv)
    near, far = exchange(near, far)
    return run_sublayer(
        1, 0, odd, temper, shifted_window, places, tails, near, far, moved, projected,
        (w_qkv, w_out, gain),
    )


def solution(mesh):
    in_specs = (
        P(("parts", "wide"), None),
        P(("parts", "wide")),
        P(("parts", "wide")),
        P(("parts", "wide")),
        P(),
        P(),
        P(),
        P(),
    )
    out_specs = P(("parts", "wide"), None)
    return jax.shard_map(body, mesh=mesh, in_specs=in_specs, out_specs=out_specs, check_vma=False)
```
